512 devices in a mesh: ctx: 16 (over y_hi, x, core), fsdp: 32 (over z, y_lo).
Axes of the slice: x: 4, y: 4 (y_hi: 2, y_lo: 2; y = y_hi * 2 + y_lo), z: 16, core: 2. Of those that a mesh axis runs over, the one named last changes fastest.
Arguments:
- tokens: bfloat16 [32, 4096, 2048], P('fsdp', 'ctx'), may hold values from -32 to 32
- query_weight: bfloat16 [2048, 512], P('fsdp'), may hold values from -0.125 to 0.125
- key_weight: bfloat16 [2048, 512], P('fsdp'), may hold values from -0.125 to 0.125
- value_weight: bfloat16 [2048, 512], P('fsdp'), may hold values from -0.125 to 0.125
- cotangent: bfloat16 [32, 4096, 512], P('fsdp', 'ctx'), may hold values from -0.29882812 to 0.29882812
- rand_owner: int32 [32, 64, 3], P('fsdp'), may hold values from 0 to 15, all different within a row; in each aligned block of 4 rows (0 to 3, 4 to 7, ..., all dimensions but the last counted through in order) at most 2 rows name the same one
- rand_offset: int32 [32, 64, 3], P('fsdp'), may hold values from 0 to 3
- global_ids: int32 [32, 2], P('fsdp'), may hold values from 0 to 63
Outputs:
- attn_out: bfloat16 [32, 4096, 512], P('fsdp', 'ctx')
- query_grad: float32 [2048, 512], P('fsdp')
The draws below stay inside these ranges and needn't reach their ends.
Inputs may be any that keep to these rules, and one draw needn't show every extreme that they name: `rand_owner`: the 3 owners named for one query block differ. The query blocks of one context shard (aligned runs of 4 blocks) take at most 2 random blocks from one owner, and exactly 2 from some owner.
All inputs are finite; a program needn't handle non-finite values.
Results may differ from the reference program's by a relative error of at most 0.015.
The reference program's roundings to bfloat16 on the way count: a program that leaves them out, or rounds other values in their place, can miss the bound.
Values may be sent and summed in bfloat16 or wider, within the bound.
No kernel may reach another device: no remote copies, remote signals or barrier semaphores. Data moves between devices by JAX's collectives and lax.ppermute only.
A program may use at most 64 MiB of HBM per device.

```python
import math
import jax
import jax.numpy as jnp
import numpy as np
from jax import lax

D = 2048
HEADS = 4
HD = 128
BLK = 64
RND = 3
GLB = 2
NBL = 4
SEQS = 32
NBLK = 64
SEQLEN = 4096
CAP = 2
N_CTX = 16


def draw_tokens(key, part):
    full_shape = (SEQS, SEQLEN, D)
    normal_part = jax.random.normal(jax.random.fold_in(key, 1), full_shape, jnp.float32)
    return jnp.clip(normal_part, -6.0, 6.0).astype(jnp.bfloat16)


def with_ends(entries, rng, low, high):
    longest = entries.shape.index(max(entries.shape))
    spots = []
    for shift in (0, 1):
        where = [jax.random.randint(jax.random.fold_in(rng, axis), (), 0, length) for axis, length in enumerate(entries.shape)]
        where[longest] = (where[longest] + shift) % entries.shape[longest]
        spots.append(tuple(where))
    return entries.at[spots[0]].set(low).at[spots[1]].set(high)


def block_levels(key, dims, split, least, high):
    def one(axis_at, blocks):
        heights = jax.random.uniform(jax.random.fold_in(jax.random.fold_in(key, 6), axis_at), (blocks,), jnp.float32, least / len(split), high / len(split))
        return jnp.repeat(jnp.exp(heights), dims[axis_at] // blocks).reshape((-1,) + (1,) * (len(dims) - axis_at - 1))

    loudness = one(*split[0])
    for cut in split[1:]:
        loudness = loudness * one(*cut)
    return loudness


def deal_out(own_key, own, number, rows, amount, top, most, skew):
    sequence = jax.random.permutation(own_key, amount)
    crowded, ordinary = load_shares(amount, rows * top, most, skew, True), load_shares(amount, rows * top, most, skew, False)
    places = jnp.arange(amount)

    def named(sizes, turn):
        used = int((sizes > 0).sum())
        fixed = max(1, used // 4)
        moved = fixed + (places - fixed + turn * (used - fixed)) % max(1, amount - fixed)
        return jnp.zeros((amount,), jnp.int32).at[sequence[jnp.where(places < fixed, places, moved)]].set(jnp.asarray(sizes, jnp.int32))

    sizes = jnp.where(number % 4 == 0, named(crowded, number // 4), named(ordinary, number - number // 4 - 1))
    mixed = jax.random.permutation(jax.random.fold_in(own, 3), amount)
    source_of, taker = mixed[0:amount // 2 * 2:2], mixed[1:amount // 2 * 2:2]
    slack = jnp.minimum(sizes[source_of] - 1, most - sizes[taker]) // 2
    slack = jnp.where((source_of == sequence[0]) | (taker == sequence[0]) | (sizes[taker] == 0), 0, jnp.maximum(slack, 0))
    moved = jax.random.randint(jax.random.fold_in(own, 4), (amount // 2,), 0, 1 << 20) % (slack + 1)
    sizes = sizes.at[source_of].add(-moved).at[taker].add(moved)
    items = jnp.searchsorted(jnp.cumsum(sizes), jnp.arange(rows * top), side="right").astype(jnp.int32)
    table = items.reshape(top, rows).T
    table = table[jax.random.permutation(jax.random.fold_in(own, 1), rows)]
    turn = jax.random.randint(jax.random.fold_in(own, 2), (rows, 1), 0, top)
    return jnp.take_along_axis(table, (jnp.arange(top)[None, :] + turn) % top, axis=1)


def load_shares(amount, total, most, slope, full):
    weights = [(1 << 20) // math.isqrt(rank ** slope) + 1 for rank in range(1, amount + 1)]
    largest = most if full else min(most, max(-(-total // amount), total * weights[0] // sum(weights)))
    least = 1 if total - largest >= amount - 1 else 0
    counts, spare = [largest] + [least] * (amount - 1), total - largest - least * (amount - 1)
    while spare > 0:
        movable = [i for i in range(1, amount) if counts[i] < largest] or [i for i in range(1, amount) if counts[i] < most]
        mass, budget = sum([weights[i] for i in movable]), spare
        for i in movable:
            addition = min(most - counts[i], max(1, budget * weights[i] // mass), spare)
            counts[i] = counts[i] + addition
            spare = spare - addition
    return np.array(counts)


def bell_draw(key, extent, scale, limit, split=(), held_as=jnp.bfloat16):
    drawn = jax.random.normal(key, extent, jnp.float32) * scale
    if len(split) > 0:
        drawn = block_levels(key, extent, split, -0.22, 0.18) * drawn
    return jnp.clip(drawn, min=-limit, max=limit).astype(held_as)


def setup_inputs(seed: int = 0) -> dict:
    key_of = jax.random.split(jax.random.key(seed), 9)
    tokens = draw_tokens(jax.random.fold_in(key_of[8], 71), 0)
    query_weight = bell_draw(key_of[1], (D, HEADS * HD), D ** -0.5, 0.125, ((0, 32),))
    key_weight = bell_draw(key_of[2], (D, HEADS * HD), D ** -0.5, 0.125, ((0, 32),))
    value_weight = bell_draw(key_of[3], (D, HEADS * HD), D ** -0.5, 0.125, ((0, 32),))
    cotangent = bell_draw(key_of[4], (SEQS, SEQLEN, HEADS * HD), 0.05, 0.29882812, ((0, 32), (1, 16)))
    rand_owner_keys = jax.random.split(jax.random.fold_in(key_of[5], 1), SEQS * NBLK // NBL)
    rand_owner_turns = jax.random.permutation(jax.random.fold_in(key_of[5], 3), SEQS * NBLK // NBL)
    rand_owner = jax.vmap(lambda own, number: deal_out(jax.random.fold_in(key_of[5], 2), own, number, NBL, N_CTX, RND, CAP, 2))(rand_owner_keys, rand_owner_turns).reshape((SEQS, NBLK, RND))
    rand_offset = with_ends(jax.random.randint(key_of[6], (SEQS, NBLK, RND), 0, NBL), jax.random.fold_in(key_of[6], 1), 0, NBL - 1).astype(jnp.int32)
    global_ids = with_ends(jax.random.randint(key_of[7], (SEQS, GLB), 0, NBLK), jax.random.fold_in(key_of[7], 1), 0, NBLK - 1).astype(jnp.int32)
    return {"tokens": tokens, "query_weight": query_weight, "key_weight": key_weight, "value_weight": value_weight, "cotangent": cotangent, "rand_owner": rand_owner, "rand_offset": rand_offset, "global_ids": global_ids}


def reference(tokens, query_weight, key_weight, value_weight, cotangent, rand_owner, rand_offset, global_ids):
    total_blocks = NBL * N_CTX
    feature_width = HEADS * HD
    score_scale = HD ** -0.5
    key_count = (3 + RND) * BLK
    masked_score = -1.0e30

    def project(inputs, weight):
        return jnp.dot(inputs, weight, preferred_element_type=jnp.float32).astype(jnp.bfloat16)

    def key_sets(matrix, chosen, global_list):
        blocks = matrix.reshape(total_blocks, BLK, feature_width)
        zero_block = jnp.zeros((1, BLK, feature_width), jnp.bfloat16)
        padded = jnp.concatenate([zero_block, blocks, zero_block], axis=0)
        window = jnp.stack([padded[:-2], padded[1:-1], padded[2:]], axis=1)
        randoms = blocks[chosen]
        local_part = jnp.concatenate([window, randoms], axis=1).reshape(total_blocks, key_count, HEADS, HD)
        global_part = blocks[global_list].reshape(GLB * BLK, HEADS, HD)
        return local_part.astype(jnp.float32), global_part.astype(jnp.float32)

    def one_sequence(running, items):
        inputs, grad_out, owners, offsets, global_list = items
        queries = project(inputs, query_weight)
        keys = project(inputs, key_weight)
        values = project(inputs, value_weight)
        chosen = (owners * NBL + offsets).astype(jnp.int32)
        local_keys, global_keys = key_sets(keys, chosen, global_list)
        local_values, global_values = key_sets(values, chosen, global_list)
        query_heads = queries.reshape(total_blocks, BLK, HEADS, HD).astype(jnp.float32)
        scores = jnp.concatenate([
            jnp.einsum('nqhd,nkhd->nhqk', query_heads, local_keys),
            jnp.einsum('nqhd,khd->nhqk', query_heads, global_keys)], axis=-1) * score_scale
        block_ids = jnp.arange(total_blocks, dtype=jnp.int32)
        left_ok = block_ids > 0
        right_ok = block_ids < total_blocks - 1
        key_valid = jnp.concatenate([
            jnp.repeat(left_ok[:, None], BLK, axis=1),
            jnp.ones((total_blocks, BLK), bool),
            jnp.repeat(right_ok[:, None], BLK, axis=1),
            jnp.ones((total_blocks, (RND + GLB) * BLK), bool)], axis=1)
        scores = jnp.where(key_valid[:, None, None, :], scores, masked_score)
        row_max = jnp.max(scores, axis=-1, keepdims=True)
        exponent = jnp.exp(scores - row_max)
        probabilities = exponent / jnp.sum(exponent, axis=-1, keepdims=True)
        weights = probabilities.astype(jnp.bfloat16).astype(jnp.float32)
        summed = jnp.einsum('nhqk,nkhd->nqhd', weights[..., :key_count], local_values)
        summed = summed + jnp.einsum('nhqk,khd->nqhd', weights[..., key_count:], global_values)
        attended = summed.reshape(SEQLEN, feature_width).astype(jnp.bfloat16)
        grad_heads = grad_out.reshape(total_blocks, BLK, HEADS, HD).astype(jnp.float32)
        grad_probs = jnp.concatenate([
            jnp.einsum('nqhd,nkhd->nhqk', grad_heads, local_values),
            jnp.einsum('nqhd,khd->nhqk', grad_heads, global_values)], axis=-1)
        row_delta = jnp.sum(probabilities * grad_probs, axis=-1, keepdims=True)
        grad_scores = (probabilities * (grad_probs - row_delta) * score_scale).astype(jnp.bfloat16).astype(jnp.float32)
        grad_query = jnp.einsum('nhqk,nkhd->nqhd', grad_scores[..., :key_count], local_keys)
        grad_query = grad_query + jnp.einsum('nhqk,khd->nqhd', grad_scores[..., key_count:], global_keys)
        grad_query = grad_query.reshape(SEQLEN, feature_width).astype(jnp.bfloat16)
        running = running + jnp.dot(inputs.T, grad_query, preferred_element_type=jnp.float32)
        return running, attended

    start_grad = jnp.zeros((D, feature_width), jnp.float32)
    query_grad, attn_out = lax.scan(one_sequence, start_grad, (tokens, cotangent, rand_owner, rand_offset, global_ids))
    return attn_out, query_grad
```

```python
import jax
import jax.numpy as jnp
from jax import lax
from jax.experimental import pallas as pl
from jax.experimental.pallas import tpu as pltpu
from jax.sharding import Mesh
from jax.sharding import PartitionSpec as P

HD = 128
BLK = 64
RND = 3
GLB = 2
NBL = 4
CHIP_BLOCKS = 8
CHIPS = 8
MASKED = -1e30

NT = (((1,), (1,)), ((), ()))
NN = (((1,), (0,)), ((), ()))
TN = (((0,), (0,)), ((), ()))


def dot32(a, b, dims):
    return lax.dot_general(a, b, dims, preferred_element_type=jnp.float32)


def spread(block, axes):
    count = lax.axis_size(axes)
    return lax.all_to_all(
        jnp.broadcast_to(block[None], (count, *block.shape)), axes, 0, 0, tiled=True
    )


def shifted(block, axis, step):
    count = lax.axis_size(axis)
    return lax.ppermute(block, axis, [(i, (i + step) % count) for i in range(count)])


def attention_kernel(
    where_ref, owner_ref, offset_ref, global_ref, q_ref, g_ref, *rest
):
    pieces, (out_ref, gq_ref, kv_ref, sems) = rest[:CHIPS], rest[CHIPS:]
    copies = [
        pltpu.make_async_copy(
            piece, kv_ref.at[pl.ds(slot * CHIP_BLOCKS, CHIP_BLOCKS)], sems.at[slot]
        )
        for slot, piece in enumerate(pieces)
    ]
    for copy in copies:
        copy.start()
    my_yh, my_x, my_core = where_ref[0], where_ref[1], where_ref[2]
    my_chip = my_yh * 4 + my_x

    def place(block):
        chip = block // CHIP_BLOCKS
        inside = lax.rem(block, CHIP_BLOCKS)
        inside = lax.rem(inside + NBL * my_core, CHIP_BLOCKS)
        hop = lax.rem(chip + 4 - my_x, 4)
        side = jnp.where(chip // 4 == my_yh, 0, 1)
        return (side * 4 + hop) * CHIP_BLOCKS + inside

    for copy in copies:
        copy.wait()

    lane = lax.broadcasted_iota(jnp.int32, (1, 2 * BLK), 1)
    total = CHIPS * CHIP_BLOCKS
    scale = HD**-0.5

    def one_block(local, carry):
        inside = lax.rem(local + NBL * my_core, CHIP_BLOCKS)
        block = my_chip * CHIP_BLOCKS + inside
        left = jnp.maximum(block - 1, 0)
        right = jnp.minimum(block + 1, total - 1)
        named = [left, right, block]
        for r in range(RND):
            named.append(owner_ref[block, r] * NBL + offset_ref[block, r])
        for r in range(GLB):
            named.append(global_ref[0, r])
        spots = [place(b) for b in named]
        kv = jnp.concatenate([kv_ref[s] for s in spots], axis=0)
        allowed = ((lane < BLK) & (block > 0)) | ((lane >= BLK) & (block < total - 1))
        rows = pl.ds(pl.multiple_of(local * BLK, BLK), BLK)
        for h in range(2):
            cols = slice(h * HD, (h + 1) * HD)
            q = q_ref[rows, cols]
            g = g_ref[rows, cols]
            k = kv[:, h * HD : (h + 1) * HD]
            v = kv[:, (2 + h) * HD : (3 + h) * HD]
            s = dot32(q, k, NT) * scale
            s = jnp.concatenate(
                [jnp.where(allowed, s[:, : 2 * BLK], MASKED), s[:, 2 * BLK :]], axis=1
            )
            e = jnp.exp(s - jnp.max(s, axis=1, keepdims=True))
            p = e / jnp.sum(e, axis=1, keepdims=True)
            out_ref[rows, cols] = dot32(p.astype(jnp.bfloat16), v, NN).astype(
                jnp.bfloat16
            )
            gp = dot32(g, v, NT)
            delta = jnp.sum(p * gp, axis=1, keepdims=True)
            ds = (p * (gp - delta) * scale).astype(jnp.bfloat16)
            gq_ref[rows, cols] = dot32(ds, k, NN).astype(jnp.bfloat16)
        return carry

    lax.fori_loop(0, CHIP_BLOCKS, one_block, 0)


def attention(where, owners, offsets, global_list, queries, grads, pieces):
    rows, width = queries.shape
    smem = pl.BlockSpec(memory_space=pltpu.SMEM)
    vmem = pl.BlockSpec(memory_space=pltpu.VMEM)
    return pl.pallas_call(
        attention_kernel,
        out_shape=(
            jax.ShapeDtypeStruct((rows, width), jnp.bfloat16),
            jax.ShapeDtypeStruct((rows, width), jnp.bfloat16),
        ),
        in_specs=[smem] * 4 + [vmem] * 2 + [pl.BlockSpec(memory_space=pl.ANY)] * CHIPS,
        out_specs=(vmem, vmem),
        scratch_shapes=[
            pltpu.VMEM((CHIPS * CHIP_BLOCKS, BLK, 2 * width), jnp.bfloat16),
            pltpu.SemaphoreType.DMA((CHIPS,)),
        ],
        compiler_params=pltpu.CompilerParams(vmem_limit_bytes=24 * 1024 * 1024),
        name="attention",
    )(where, owners, offsets, global_list, queries, grads, *pieces)


def per_device(
    tokens, query_weight, key_weight, value_weight, cotangent, rand_owner, rand_offset, global_ids
):
    own = tokens[0]
    grad_out = cotangent[0]
    yh, x, core = lax.axis_index("yh"), lax.axis_index("x"), lax.axis_index("core")
    part = yh * 4 + x
    half = query_weight.shape[1] // 2

    other = shifted(own, "core", 1)
    grads_mine = lax.dynamic_slice_in_dim(grad_out, core * half, half, 1)
    grads_send = lax.dynamic_slice_in_dim(grad_out, (1 - core) * half, half, 1)
    grads = jnp.concatenate([grads_mine, shifted(grads_send, "core", 1)], axis=0)

    rows = query_weight.shape[0] // 8
    weight_part = jnp.concatenate(
        [
            lax.dynamic_slice(w, (part * rows, core * half), (rows, half))
            for w in (key_weight, value_weight, query_weight)
        ],
        axis=1,
    )
    weight = spread(weight_part, "z").reshape(16, rows, 3 * half)
    weight = spread(weight, ("yh", "yl"))
    weight = spread(weight, "x")
    weight = weight.reshape(4, 2, 2, 16, rows, 3 * half)
    weight = weight.transpose(3, 2, 1, 0, 4, 5).reshape(-1, 3 * half)

    def project(inputs):
        return dot32(inputs, weight, NN).astype(jnp.bfloat16)

    mine, theirs = project(own), project(other)
    kv = jnp.concatenate([mine[:, : 2 * half], theirs[:, : 2 * half]], axis=0)
    queries = jnp.concatenate([mine[:, 2 * half :], theirs[:, 2 * half :]], axis=0)
    kv = kv.reshape(CHIP_BLOCKS, BLK, 2 * half)
    across = shifted(kv, "yh", 1)
    pieces = []
    for block in (kv, across):
        before, after = shifted(block, "x", 1), shifted(block, "x", -1)
        cut = CHIP_BLOCKS // 2
        far = jnp.concatenate(
            [shifted(before[:cut], "x", 1), shifted(after[cut:], "x", -1)], axis=0
        )
        pieces += [block, after, far, before]

    where = jnp.stack([yh, x, core]).astype(jnp.int32)
    attended, grad_query = attention(
        where, rand_owner[0], rand_offset[0], global_ids, queries, grads, pieces
    )
    count = own.shape[0]
    out_back = shifted(attended[count:], "core", 1)
    out_mine = attended[:count]
    attn = jnp.where(
        core == 0,
        jnp.concatenate([out_mine, out_back], axis=1),
        jnp.concatenate([out_back, out_mine], axis=1),
    )

    partial = dot32(own, grad_query[:count], TN) + dot32(other, grad_query[count:], TN)
    partial = partial.astype(jnp.bfloat16).reshape(16, 2, 2, 4, rows, half)
    partial = partial.transpose(1, 2, 3, 0, 4, 5).reshape(16, 16 * rows, half)
    partial = lax.all_to_all(partial, ("yl", "yh", "x"), 0, 0, tiled=True)
    partial = jnp.sum(partial.astype(jnp.float32), axis=0).astype(jnp.bfloat16)
    partial = lax.all_to_all(partial.reshape(16, rows, half), "z", 0, 0, tiled=True)
    partial = jnp.sum(partial.astype(jnp.float32), axis=0)
    final = spread(partial, ("yh", "x", "core")).reshape(8, 2, rows, half)
    query_grad = final.transpose(0, 2, 1, 3).reshape(8 * rows, 2 * half)
    return attn[None], query_grad


def solution(mesh):
    fine = Mesh(
        mesh.devices.reshape(2, 4, 2, 16, 2),
        ("yh", "x", "core", "z", "yl"),
        axis_types=(jax.sharding.AxisType.Auto,) * 5,
    )
    ctx, fsdp = ("yh", "x", "core"), ("z", "yl")
    placed = (
        P(fsdp, ctx, None),
        P(fsdp, None),
        P(fsdp, None),
        P(fsdp, None),
        P(fsdp, ctx, None),
        P(fsdp, None, None),
        P(fsdp, None, None),
        P(fsdp, None),
    )
    return jax.shard_map(
        per_device,
        mesh=fine,
        in_specs=placed,
        out_specs=(P(fsdp, ctx, None), P(fsdp, None)),
        check_vma=False,
    )
```

```python
import jax
import jax.numpy as jnp
from jax import lax
from jax.experimental import pallas as pl
from jax.experimental.pallas import tpu as pltpu
from jax.sharding import Mesh
from jax.sharding import PartitionSpec as P

HD = 128
BLK = 64
RND = 3
GLB = 2
NBL = 4
PIECE_BLOCKS = 16
PIECES = 4
HEADS = 4
MASKED = -1e30

NT = (((1,), (1,)), ((), ()))
NN = (((1,), (0,)), ((), ()))
TN = (((0,), (0,)), ((), ()))


def dot32(a, b, dims):
    return lax.dot_general(a, b, dims, preferred_element_type=jnp.float32)


def spread(block, axes):
    count = lax.axis_size(axes)
    return lax.all_to_all(
        jnp.broadcast_to(block[None], (count, *block.shape)), axes, 0, 0, tiled=True
    )


def shifted(block, axis, step):
    count = lax.axis_size(axis)
    return lax.ppermute(block, axis, [(i, (i + step) % count) for i in range(count)])


def attention_kernel(where_ref, owner_ref, offset_ref, global_ref, g_ref, *rest):
    q_refs, pieces = rest[:HEADS], rest[HEADS : HEADS + PIECES]
    out_ref, *gq_refs = rest[HEADS + PIECES : 2 * HEADS + PIECES + 1]
    kv_ref, sems = rest[2 * HEADS + PIECES + 1 :]
    copies = [
        pltpu.make_async_copy(
            piece, kv_ref.at[pl.ds(slot * PIECE_BLOCKS, PIECE_BLOCKS)], sems.at[slot]
        )
        for slot, piece in enumerate(pieces)
    ]
    for copy in copies:
        copy.start()
    my_yh, my_x, my_core = where_ref[0], where_ref[1], where_ref[2]

    def place(block):
        shard, inside = block // NBL, lax.rem(block, NBL)
        yh, x, core = shard // 8, lax.rem(shard // 2, 4), lax.rem(shard, 2)
        piece = jnp.where(core == my_core, 0, 1) + jnp.where(yh == my_yh, 0, 2)
        slot = lax.rem(my_x + 4 - x, 4)
        return piece * PIECE_BLOCKS + slot * NBL + inside

    for copy in copies:
        copy.wait()

    lane = lax.broadcasted_iota(jnp.int32, (1, 2 * BLK), 1)
    total = PIECES * PIECE_BLOCKS
    scale = HD**-0.5

    def one_block(slot, inside):
        x = lax.rem(my_x + 4 - slot, 4)
        block = ((my_yh * 4 + x) * 2 + my_core) * NBL + inside
        left = jnp.maximum(block - 1, 0)
        right = jnp.minimum(block + 1, total - 1)
        named = [left, right, block]
        for r in range(RND):
            named.append(owner_ref[block, r] * NBL + offset_ref[block, r])
        for r in range(GLB):
            named.append(global_ref[0, r])
        spots = [place(b) for b in named]
        kv = jnp.concatenate([kv_ref[s] for s in spots], axis=0)
        k, v = kv[:, :HD], kv[:, HD:]
        allowed = ((lane < BLK) & (block > 0)) | ((lane >= BLK) & (block < total - 1))
        rows = pl.ds(pl.multiple_of(inside * BLK, BLK), BLK)
        q = q_refs[slot][rows, :]
        g = g_ref[x, rows, :]
        s = dot32(q, k, NT) * scale
        s = jnp.concatenate(
            [jnp.where(allowed, s[:, : 2 * BLK], MASKED), s[:, 2 * BLK :]], axis=1
        )
        e = jnp.exp(s - jnp.max(s, axis=1, keepdims=True))
        p = e / jnp.sum(e, axis=1, keepdims=True)
        out_ref[x, rows, :] = dot32(p.astype(jnp.bfloat16), v, NN).astype(jnp.bfloat16)
        gp = dot32(g, v, NT)
        delta = jnp.sum(p * gp, axis=1, keepdims=True)
        ds = (p * (gp - delta) * scale).astype(jnp.bfloat16)
        gq_refs[slot][rows, :] = dot32(ds, k, NN).astype(jnp.bfloat16)

    def step(inside, carry):
        for slot in range(HEADS):
            one_block(slot, inside)
        return carry

    lax.fori_loop(0, NBL, step, 0)


def attention(where, owners, offsets, global_list, grads, queries, pieces):
    rows, width = queries[0].shape
    smem = pl.BlockSpec(memory_space=pltpu.SMEM)
    vmem = pl.BlockSpec(memory_space=pltpu.VMEM)
    return pl.pallas_call(
        attention_kernel,
        out_shape=(jax.ShapeDtypeStruct(grads.shape, jnp.bfloat16),)
        + (jax.ShapeDtypeStruct((rows, width), jnp.bfloat16),) * HEADS,
        in_specs=[smem] * 4
        + [vmem] * (1 + HEADS)
        + [pl.BlockSpec(memory_space=pl.ANY)] * PIECES,
        out_specs=(vmem,) * (1 + HEADS),
        scratch_shapes=[
            pltpu.VMEM((PIECES * PIECE_BLOCKS, BLK, 2 * width), jnp.bfloat16),
            pltpu.SemaphoreType.DMA((PIECES,)),
        ],
        compiler_params=pltpu.CompilerParams(vmem_limit_bytes=24 * 1024 * 1024),
        name="attention",
    )(where, owners, offsets, global_list, grads, *queries, *pieces)


def per_device(
    tokens, query_weight, key_weight, value_weight, cotangent, rand_owner, rand_offset, global_ids
):
    own = tokens[0]
    yh, x, core = lax.axis_index("yh"), lax.axis_index("x"), lax.axis_index("core")
    count, depth = own.shape

    before, after = shifted(own, "x", 1), shifted(own, "x", -1)
    cut = count // 2
    far = jnp.concatenate(
        [shifted(before[:cut], "x", 1), shifted(after[cut:], "x", -1)], axis=0
    )
    token_sets = (own, before, far, after)
    grads = cotangent[0].reshape(count, HEADS, HD).transpose(1, 0, 2)
    grads = lax.all_to_all(grads, "x", 0, 0, tiled=True)

    rows = query_weight.shape[0] // 4
    weight = jnp.concatenate(
        [
            lax.dynamic_slice(w, ((yh * 2 + core) * rows, x * HD), (rows, HD))
            for w in (key_weight, value_weight, query_weight)
        ],
        axis=1,
    )
    weight = spread(weight, "z").reshape(16, rows, 3 * HD)
    weight = spread(weight, ("yh", "yl")).reshape(2, 2, 16, rows, 3 * HD)
    weight = weight.transpose(2, 1, 0, 3, 4)
    partner = shifted(weight, "core", 1)
    weight = jnp.where(
        core == 0,
        jnp.stack([weight, partner], axis=3),
        jnp.stack([partner, weight], axis=3),
    ).reshape(depth, 3 * HD)

    kv = jnp.concatenate(
        [dot32(t, weight[:, : 2 * HD], NN).astype(jnp.bfloat16) for t in token_sets], axis=0
    ).reshape(PIECE_BLOCKS, BLK, 2 * HD)
    queries = [dot32(t, weight[:, 2 * HD :], NN).astype(jnp.bfloat16) for t in token_sets]
    across = shifted(kv, "yh", 1)
    pieces = [kv, shifted(kv, "core", 1), across, shifted(across, "core", 1)]

    where = jnp.stack([yh, x, core]).astype(jnp.int32)
    attended, *grad_queries = attention(
        where, rand_owner[0], rand_offset[0], global_ids, grads, queries, pieces
    )
    attn = lax.all_to_all(attended, "x", 0, 0, tiled=True)
    attn = attn.transpose(1, 0, 2).reshape(count, HEADS * HD)

    partial = sum(dot32(t, g, TN) for t, g in zip(token_sets, grad_queries))
    partial = partial.astype(jnp.bfloat16).reshape(16, 2, 2, 2, rows, HD)
    partial = partial.transpose(2, 1, 3, 0, 4, 5).reshape(8, 16 * rows, HD)
    partial = lax.all_to_all(partial, ("yh", "yl", "core"), 0, 0, tiled=True)
    partial = jnp.sum(partial.astype(jnp.float32), axis=0).astype(jnp.bfloat16)
    partial = lax.all_to_all(partial.reshape(16, rows, HD), "z", 0, 0, tiled=True)
    partial = jnp.sum(partial.astype(jnp.float32), axis=0)
    final = spread(partial, ("yh", "x", "core")).reshape(2, 4, 2, rows, HD)
    query_grad = final.transpose(0, 2, 3, 1, 4).reshape(4 * rows, HEADS * HD)
    return attn[None], query_grad


def solution(mesh):
    fine = Mesh(
        mesh.devices.reshape(2, 4, 2, 16, 2),
        ("yh", "x", "core", "z", "yl"),
        axis_types=(jax.sharding.AxisType.Auto,) * 5,
    )
    ctx, fsdp = ("yh", "x", "core"), ("z", "yl")
    placed = (
        P(fsdp, ctx, None),
        P(fsdp, None),
        P(fsdp, None),
        P(fsdp, None),
        P(fsdp, ctx, None),
        P(fsdp, None, None),
        P(fsdp, None, None),
        P(fsdp, None),
    )
    return jax.shard_map(
        per_device,
        mesh=fine,
        in_specs=placed,
        out_specs=(P(fsdp, ctx, None), P(fsdp, None)),
        check_vma=False,
    )
```

```python
import jax
import jax.numpy as jnp
from jax import lax
from jax.experimental import pallas as pl
from jax.experimental.pallas import tpu as pltpu
from jax.sharding import Mesh
from jax.sharding import PartitionSpec as P

HD = 128
BLK = 64
RND = 3
GLB = 2
NBL = 4
PIECE_BLOCKS = 16
PIECES = 4
HEADS = 4
MASKED = -1e30

NT = (((1,), (1,)), ((), ()))
NN = (((1,), (0,)), ((), ()))
TN = (((0,), (0,)), ((), ()))


def dot32(a, b, dims):
    return lax.dot_general(a, b, dims, preferred_element_type=jnp.float32)


def spread(block, axes):
    count = lax.axis_size(axes)
    return lax.all_to_all(
        jnp.broadcast_to(block[None], (count, *block.shape)), axes, 0, 0, tiled=True
    )


def shifted(block, axis, step):
    count = lax.axis_size(axis)
    return lax.ppermute(block, axis, [(i, (i + step) % count) for i in range(count)])


def slice_kernel(where_ref, key_ref, value_ref, query_ref, out_ref):
    count, rows, _ = out_ref.shape
    start = pl.multiple_of((where_ref[0] * 2 + where_ref[2]) * rows, rows)
    col = pl.multiple_of(where_ref[1] * HD, HD)
    for i, ref in enumerate((key_ref, value_ref, query_ref)):
        part = ref[pl.ds(start, rows), pl.ds(col, HD)]
        for copy in range(count):
            out_ref[copy, :, i * HD : (i + 1) * HD] = part


def project_kernel(where_ref, mine_ref, theirs_ref, *rest):
    token_refs, (q_ref, kv_ref, w_ref) = rest[:-3], rest[-3:]
    core = where_ref[2]
    _, _, depth, rows, width = mine_ref.shape

    def assemble(z, carry):
        for yl in range(2):
            for yh in range(2):
                base = (z * 2 + yl) * 4 * rows + yh * 2 * rows
                here = pl.multiple_of(base + core * rows, rows)
                there = pl.multiple_of(base + (1 - core) * rows, rows)
                w_ref[pl.ds(here, rows), :] = mine_ref[yh, yl, z]
                w_ref[pl.ds(there, rows), :] = theirs_ref[yh, yl, z]
        return carry

    lax.fori_loop(0, depth, assemble, 0)
    for slot, group in token_groups(token_refs):
        tokens = jnp.concatenate([ref[...] for ref in group], axis=0)
        size = tokens.shape[0]
        out = dot32(tokens, w_ref[...], NN).astype(jnp.bfloat16)
        kv_ref[slot * NBL : (slot + 1) * NBL] = out[:, : 2 * HD].reshape(NBL, BLK, 2 * HD)
        q_ref[slot * size : (slot + 1) * size, :] = out[:, 2 * HD :]


def token_groups(refs):
    own, before, after, low_far, high_far = refs
    return [(0, (own,)), (1, (before,)), (3, (after,)), (2, (low_far, high_far))]


def project(where, mine, theirs, token_sets):
    count, depth = token_sets[0].shape
    total = count * HEADS
    vmem = pl.BlockSpec(memory_space=pltpu.VMEM)
    return pl.pallas_call(
        project_kernel,
        out_shape=(
            jax.ShapeDtypeStruct((total, HD), jnp.bfloat16),
            jax.ShapeDtypeStruct((PIECE_BLOCKS, BLK, 2 * HD), jnp.bfloat16),
        ),
        in_specs=[pl.BlockSpec(memory_space=pltpu.SMEM)] + [vmem] * (2 + len(token_sets)),
        out_specs=(vmem, vmem),
        scratch_shapes=[pltpu.VMEM((depth, 3 * HD), jnp.bfloat16)],
        compiler_params=pltpu.CompilerParams(vmem_limit_bytes=24 * 1024 * 1024),
        name="project",
    )(where, mine, theirs, *token_sets)


def attention_kernel(where_ref, owner_ref, offset_ref, global_ref, *rest):
    given, pieces, token_refs = rest[:2], rest[2 : 2 + PIECES], rest[2 + PIECES : -8]
    out_ref, part_ref, kv_ref, g_ref, q_ref, gq_ref, t_ref, sems = rest[-8:]
    pairs = [
        (piece, kv_ref.at[pl.ds(slot * PIECE_BLOCKS, PIECE_BLOCKS)])
        for slot, piece in enumerate(pieces)
    ]
    pairs += list(zip(given, (g_ref, q_ref)))
    first = len(pairs)
    for slot, group in token_groups(token_refs):
        size = group[0].shape[0]
        pairs += [
            (ref, t_ref.at[slot, pl.ds(i * size, size)]) for i, ref in enumerate(group)
        ]
    copies = [
        pltpu.make_async_copy(source, target, sems.at[i])
        for i, (source, target) in enumerate(pairs)
    ]
    for copy in copies:
        copy.start()
    copies, later = copies[:first], copies[first:]
    my_yh, my_x, my_core = where_ref[0], where_ref[1], where_ref[2]

    def place(block):
        shard, inside = block // NBL, lax.rem(block, NBL)
        yh, x, core = shard // 8, lax.rem(shard // 2, 4), lax.rem(shard, 2)
        piece = jnp.where(core == my_core, 0, 1) + jnp.where(yh == my_yh, 0, 2)
        slot = lax.rem(my_x + 4 - x, 4)
        return piece * PIECE_BLOCKS + slot * NBL + inside

    for copy in copies:
        copy.wait()

    lane = lax.broadcasted_iota(jnp.int32, (1, 2 * BLK), 1)
    total = PIECES * PIECE_BLOCKS
    scale = HD**-0.5

    def step(inside, carry):
        rows = pl.ds(pl.multiple_of(inside * BLK, BLK), BLK)
        ks, vs, ss, gps = [], [], [], []
        for slot in range(HEADS):
            x = lax.rem(my_x + 4 - slot, 4)
            block = ((my_yh * 4 + x) * 2 + my_core) * NBL + inside
            left = jnp.maximum(block - 1, 0)
            right = jnp.minimum(block + 1, total - 1)
            named = [left, right, block]
            for r in range(RND):
                named.append(owner_ref[block, r] * NBL + offset_ref[block, r])
            for r in range(GLB):
                named.append(global_ref[0, r])
            kv = jnp.concatenate([kv_ref[place(b)] for b in named], axis=0)
            k, v = kv[:, :HD], kv[:, HD:]
            allowed = ((lane < BLK) & (block > 0)) | ((lane >= BLK) & (block < total - 1))
            place_rows = pl.ds(pl.multiple_of(slot * NBL * BLK + inside * BLK, BLK), BLK)
            s = dot32(q_ref[place_rows, :], k, NT) * scale
            s = jnp.concatenate(
                [jnp.where(allowed, s[:, : 2 * BLK], MASKED), s[:, 2 * BLK :]], axis=1
            )
            ks.append(k)
            vs.append(v)
            ss.append(s)
            gps.append(dot32(g_ref[x, rows, :], v, NT))
        for slot in range(HEADS):
            s, gp = ss[slot], gps[slot]
            e = jnp.exp(s - jnp.max(s, axis=1, keepdims=True))
            p = e * (1.0 / jnp.sum(e, axis=1, keepdims=True))
            delta = jnp.sum(p * gp, axis=1, keepdims=True)
            ds = (p * (gp - delta) * scale).astype(jnp.bfloat16)
            out_ref[slot, rows, :] = dot32(p.astype(jnp.bfloat16), vs[slot], NN).astype(
                jnp.bfloat16
            )
            gq_ref[slot, rows, :] = dot32(ds, ks[slot], NN).astype(jnp.bfloat16)
        return carry

    lax.fori_loop(0, NBL, step, 0)

    acc = None
    for copy in later:
        copy.wait()
    for slot in range(HEADS):
        term = dot32(gq_ref[slot], t_ref[slot], TN)
        acc = term if acc is None else acc + term
    rows = part_ref.shape[2]
    for z in range(16):
        turned = acc[:, z * HD : (z + 1) * HD].T.astype(jnp.bfloat16)
        for yl in range(2):
            for q in range(4):
                at = yl * 4 * rows + q * rows
                part_ref[((q // 2) * 2 + yl) * 2 + q % 2, z] = turned[at : at + rows]


def attention(where, owners, offsets, global_list, grads, queries, pieces, token_sets):
    smem = pl.BlockSpec(memory_space=pltpu.SMEM)
    vmem = pl.BlockSpec(memory_space=pltpu.VMEM)
    return pl.pallas_call(
        attention_kernel,
        out_shape=(
            jax.ShapeDtypeStruct(grads.shape, jnp.bfloat16),
            jax.ShapeDtypeStruct((8, 16, 16, HD), jnp.bfloat16),
        ),
        in_specs=[smem] * 4
        + [pl.BlockSpec(memory_space=pl.ANY)] * (2 + PIECES + len(token_sets)),
        out_specs=(vmem, vmem),
        scratch_shapes=[
            pltpu.VMEM((PIECES * PIECE_BLOCKS, BLK, 2 * HD), jnp.bfloat16),
            pltpu.VMEM(grads.shape, jnp.bfloat16),
            pltpu.VMEM(queries.shape, jnp.bfloat16),
            pltpu.VMEM(grads.shape, jnp.bfloat16),
            pltpu.VMEM((HEADS, *token_sets[0].shape), jnp.bfloat16),
            pltpu.SemaphoreType.DMA((2 + PIECES + len(token_sets),)),
        ],
        compiler_params=pltpu.CompilerParams(vmem_limit_bytes=32 * 1024 * 1024),
        name="attention",
    )(where, owners, offsets, global_list, grads, queries, *pieces, *token_sets)


def merge_kernel(where_ref, *refs):
    out_ref = refs[-1]
    for slot, ref in enumerate(refs[:-1]):
        head = lax.rem(where_ref[1] + slot, HEADS)
        out_ref[:, pl.ds(pl.multiple_of(head * HD, HD), HD)] = ref[...]


def per_device(
    tokens, query_weight, key_weight, value_weight, cotangent, rand_owner, rand_offset, global_ids
):
    own = tokens[0]
    count, depth = own.shape
    where = jnp.stack(
        [lax.axis_index("yh"), lax.axis_index("x"), lax.axis_index("core")]
    ).astype(jnp.int32)
    smem = pl.BlockSpec(memory_space=pltpu.SMEM)
    vmem = pl.BlockSpec(memory_space=pltpu.VMEM)

    rows = query_weight.shape[0] // 4
    weight = pl.pallas_call(
        slice_kernel,
        out_shape=jax.ShapeDtypeStruct((16, rows, 3 * HD), jnp.bfloat16),
        in_specs=[smem] + [vmem] * 3,
        out_specs=vmem,
        name="slice",
    )(where, key_weight, value_weight, query_weight)
    weight = lax.all_to_all(weight, "z", 0, 0, tiled=True)
    weight = spread(weight, ("yh", "yl")).reshape(2, 2, 16, rows, 3 * HD)
    partner = shifted(weight, "core", 1)

    cut = count // 2
    before, after = shifted(own, "x", 1), shifted(own, "x", -1)
    low_far, high_far = shifted(before[:cut], "x", 1), shifted(after[cut:], "x", -1)
    token_sets = (own, before, after, low_far, high_far)
    grads = cotangent[0].reshape(count, HEADS, HD).transpose(1, 0, 2)
    grads = lax.all_to_all(grads, "x", 0, 0, tiled=True)

    queries, kv = project(where, weight, partner, token_sets)
    across = shifted(kv, "yh", 1)
    across, grads = lax.optimization_barrier((across, grads))
    pieces = [kv, shifted(kv, "core", 1), across, shifted(across, "core", 1)]

    attended, partial = attention(
        where, rand_owner[0], rand_offset[0], global_ids, grads, queries, pieces, token_sets
    )
    returned = [attended[0]] + [shifted(attended[s], "x", -s) for s in range(1, HEADS)]
    attn = pl.pallas_call(
        merge_kernel,
        out_shape=jax.ShapeDtypeStruct((count, HEADS * HD), jnp.bfloat16),
        in_specs=[smem] + [vmem] * HEADS,
        out_specs=vmem,
        name="merge",
    )(where, *returned)

    partial = lax.all_to_all(partial, ("yh", "yl", "core"), 0, 0, tiled=True)
    partial = jnp.sum(partial.astype(jnp.float32), axis=0).astype(jnp.bfloat16)
    partial, attn = lax.optimization_barrier((partial, attn))
    partial = lax.all_to_all(partial, "z", 0, 0, tiled=True)
    partial = jnp.sum(partial.astype(jnp.float32), axis=0)
    final = spread(partial, ("yh", "x", "core")).reshape(2, 4, 2, rows, HD)
    query_grad = final.transpose(0, 2, 3, 1, 4).reshape(4 * rows, HEADS * HD)
    return attn[None], query_grad


def solution(mesh):
    fine = Mesh(
        mesh.devices.reshape(2, 4, 2, 16, 2),
        ("yh", "x", "core", "z", "yl"),
        axis_types=(jax.sharding.AxisType.Auto,) * 5,
    )
    ctx, fsdp = ("yh", "x", "core"), ("z", "yl")
    placed = (
        P(fsdp, ctx, None),
        P(fsdp, None),
        P(fsdp, None),
        P(fsdp, None),
        P(fsdp, ctx, None),
        P(fsdp, None, None),
        P(fsdp, None, None),
        P(fsdp, None),
    )
    return jax.shard_map(
        per_device,
        mesh=fine,
        in_specs=placed,
        out_specs=(P(fsdp, ctx, None), P(fsdp, None)),
        check_vma=False,
    )
```

```python
import jax
import jax.numpy as jnp
from jax import lax
from jax.experimental import pallas as pl
from jax.experimental.pallas import tpu as pltpu
from jax.sharding import Mesh
from jax.sharding import PartitionSpec as P

HD = 128
BLK = 64
RND = 3
GLB = 2
NBL = 4
PIECE_BLOCKS = 16
PIECES = 4
HEADS = 4
MASKED = -1e30

NT = (((1,), (1,)), ((), ()))
NN = (((1,), (0,)), ((), ()))
TN = (((0,), (0,)), ((), ()))


def dot32(a, b, dims):
    return lax.dot_general(a, b, dims, preferred_element_type=jnp.float32)


def spread(block, axes):
    count = lax.axis_size(axes)
    return lax.all_to_all(
        jnp.broadcast_to(block[None], (count, *block.shape)), axes, 0, 0, tiled=True
    )


def shifted(block, axis, step):
    count = lax.axis_size(axis)
    return lax.ppermute(block, axis, [(i, (i + step) % count) for i in range(count)])


def slice_kernel(where_ref, key_ref, value_ref, query_ref, out_ref):
    count, rows, _ = out_ref.shape
    start = pl.multiple_of((where_ref[0] * 2 + where_ref[2]) * rows, rows)
    col = pl.multiple_of(where_ref[1] * HD, HD)
    for i, ref in enumerate((key_ref, value_ref, query_ref)):
        part = ref[pl.ds(start, rows), pl.ds(col, HD)]
        for copy in range(count):
            out_ref[copy, :, i * HD : (i + 1) * HD] = part


def project_kernel(where_ref, mine_ref, theirs_a_ref, theirs_b_ref, *rest):
    theirs = (theirs_a_ref, theirs_b_ref)
    token_refs, (q_ref, kv_ref, w_ref) = rest[:-3], rest[-3:]
    core = where_ref[2]
    _, _, depth, rows, width = mine_ref.shape

    def assemble(z, carry):
        for yl in range(2):
            for yh in range(2):
                base = (z * 2 + yl) * 4 * rows + yh * 2 * rows
                here = pl.multiple_of(base + core * rows, rows)
                there = pl.multiple_of(base + (1 - core) * rows, rows)
                w_ref[pl.ds(here, rows), :] = mine_ref[yh, yl, z]
                w_ref[pl.ds(there, rows), :] = theirs[yh][yl, z]
        return carry

    lax.fori_loop(0, depth, assemble, 0)
    for slot, group in token_groups(token_refs):
        tokens = jnp.concatenate([ref[...] for ref in group], axis=0)
        size = tokens.shape[0]
        out = dot32(tokens, w_ref[...], NN).astype(jnp.bfloat16)
        kv_ref[slot * NBL : (slot + 1) * NBL] = out[:, : 2 * HD].reshape(NBL, BLK, 2 * HD)
        q_ref[slot * size : (slot + 1) * size, :] = out[:, 2 * HD :]


def token_groups(refs):
    own, before, after, low_far, high_far = refs
    return [(0, (own,)), (1, (before,)), (3, (after,)), (2, (low_far, high_far))]


def project(where, mine, theirs_a, theirs_b, token_sets):
    count, depth = token_sets[0].shape
    total = count * HEADS
    vmem = pl.BlockSpec(memory_space=pltpu.VMEM)
    return pl.pallas_call(
        project_kernel,
        out_shape=(
            jax.ShapeDtypeStruct((total, HD), jnp.bfloat16),
            jax.ShapeDtypeStruct((PIECE_BLOCKS, BLK, 2 * HD), jnp.bfloat16),
        ),
        in_specs=[pl.BlockSpec(memory_space=pltpu.SMEM)] + [vmem] * (3 + len(token_sets)),
        out_specs=(vmem, vmem),
        scratch_shapes=[pltpu.VMEM((depth, 3 * HD), jnp.bfloat16)],
        compiler_params=pltpu.CompilerParams(vmem_limit_bytes=24 * 1024 * 1024),
        name="project",
    )(where, mine, theirs_a, theirs_b, *token_sets)


def attention_kernel(where_ref, owner_ref, offset_ref, global_ref, *rest):
    given, pieces, token_refs = rest[:2], rest[2 : 2 + PIECES], rest[2 + PIECES : -8]
    out_ref, part_ref, kv_ref, g_ref, q_ref, gq_ref, t_ref, sems = rest[-8:]
    pairs = [
        (piece, kv_ref.at[pl.ds(slot * PIECE_BLOCKS, PIECE_BLOCKS)])
        for slot, piece in enumerate(pieces)
    ]
    pairs += list(zip(given, (g_ref, q_ref)))
    first = len(pairs)
    for slot, group in token_groups(token_refs):
        size = group[0].shape[0]
        pairs += [
            (ref, t_ref.at[slot, pl.ds(i * size, size)]) for i, ref in enumerate(group)
        ]
    copies = [
        pltpu.make_async_copy(source, target, sems.at[i])
        for i, (source, target) in enumerate(pairs)
    ]
    for copy in copies:
        copy.start()
    copies, later = copies[:first], copies[first:]
    my_yh, my_x, my_core = where_ref[0], where_ref[1], where_ref[2]

    def place(block):
        shard, inside = block // NBL, lax.rem(block, NBL)
        yh, x, core = shard // 8, lax.rem(shard // 2, 4), lax.rem(shard, 2)
        piece = jnp.where(core == my_core, 0, 1) + jnp.where(yh == my_yh, 0, 2)
        slot = lax.rem(my_x + 4 - x, 4)
        return piece * PIECE_BLOCKS + slot * NBL + inside

    for copy in copies:
        copy.wait()

    lane = lax.broadcasted_iota(jnp.int32, (1, 2 * BLK), 1)
    total = PIECES * PIECE_BLOCKS
    scale = HD**-0.5

    def step(inside, carry):
        rows = pl.ds(pl.multiple_of(inside * BLK, BLK), BLK)
        ks, vs, ss, gps = [], [], [], []
        for slot in range(HEADS):
            x = lax.rem(my_x + 4 - slot, 4)
            block = ((my_yh * 4 + x) * 2 + my_core) * NBL + inside
            left = jnp.maximum(block - 1, 0)
            right = jnp.minimum(block + 1, total - 1)
            named = [left, right, block]
            for r in range(RND):
                named.append(owner_ref[block, r] * NBL + offset_ref[block, r])
            for r in range(GLB):
                named.append(global_ref[0, r])
            kv = jnp.concatenate([kv_ref[place(b)] for b in named], axis=0)
            k, v = kv[:, :HD], kv[:, HD:]
            allowed = ((lane < BLK) & (block > 0)) | ((lane >= BLK) & (block < total - 1))
            place_rows = pl.ds(pl.multiple_of(slot * NBL * BLK + inside * BLK, BLK), BLK)
            s = dot32(q_ref[place_rows, :], k, NT) * scale
            s = jnp.concatenate(
                [jnp.where(allowed, s[:, : 2 * BLK], MASKED), s[:, 2 * BLK :]], axis=1
            )
            ks.append(k)
            vs.append(v)
            ss.append(s)
            gps.append(dot32(g_ref[x, rows, :], v, NT))
        for slot in range(HEADS):
            s, gp = ss[slot], gps[slot]
            e = jnp.exp(s - jnp.max(s, axis=1, keepdims=True))
            p = e * (1.0 / jnp.sum(e, axis=1, keepdims=True))
            delta = jnp.sum(p * gp, axis=1, keepdims=True)
            ds = (p * (gp - delta) * scale).astype(jnp.bfloat16)
            out_ref[slot, rows, :] = dot32(p.astype(jnp.bfloat16), vs[slot], NN).astype(
                jnp.bfloat16
            )
            gq_ref[slot, rows, :] = dot32(ds, ks[slot], NN).astype(jnp.bfloat16)
        return carry

    lax.fori_loop(0, NBL, step, 0)

    acc = None
    for copy in later:
        copy.wait()
    for slot in range(HEADS):
        term = dot32(gq_ref[slot], t_ref[slot], TN)
        acc = term if acc is None else acc + term
    rows = part_ref.shape[2]
    for z in range(16):
        turned = acc[:, z * HD : (z + 1) * HD].T.astype(jnp.bfloat16)
        for yl in range(2):
            for q in range(4):
                at = yl * 4 * rows + q * rows
                part_ref[((q // 2) * 2 + yl) * 2 + q % 2, z] = turned[at : at + rows]


def attention(where, owners, offsets, global_list, grads, queries, pieces, token_sets):
    smem = pl.BlockSpec(memory_space=pltpu.SMEM)
    vmem = pl.BlockSpec(memory_space=pltpu.VMEM)
    return pl.pallas_call(
        attention_kernel,
        out_shape=(
            jax.ShapeDtypeStruct(grads.shape, jnp.bfloat16),
            jax.ShapeDtypeStruct((8, 16, 16, HD), jnp.bfloat16),
        ),
        in_specs=[smem] * 4
        + [pl.BlockSpec(memory_space=pl.ANY)] * (2 + PIECES + len(token_sets)),
        out_specs=(vmem, vmem),
        scratch_shapes=[
            pltpu.VMEM((PIECES * PIECE_BLOCKS, BLK, 2 * HD), jnp.bfloat16),
            pltpu.VMEM(grads.shape, jnp.bfloat16),
            pltpu.VMEM(queries.shape, jnp.bfloat16),
            pltpu.VMEM(grads.shape, jnp.bfloat16),
            pltpu.VMEM((HEADS, *token_sets[0].shape), jnp.bfloat16),
            pltpu.SemaphoreType.DMA((2 + PIECES + len(token_sets),)),
        ],
        compiler_params=pltpu.CompilerParams(vmem_limit_bytes=56 * 1024 * 1024),
        name="attention",
    )(where, owners, offsets, global_list, grads, queries, *pieces, *token_sets)


def merge_kernel(where_ref, *refs):
    out_ref = refs[-1]
    for slot, ref in enumerate(refs[:-1]):
        head = lax.rem(where_ref[1] + slot, HEADS)
        out_ref[:, pl.ds(pl.multiple_of(head * HD, HD), HD)] = ref[...]


def per_device(
    tokens, query_weight, key_weight, value_weight, cotangent, rand_owner, rand_offset, global_ids
):
    own = tokens[0]
    count, depth = own.shape
    where = jnp.stack(
        [lax.axis_index("yh"), lax.axis_index("x"), lax.axis_index("core")]
    ).astype(jnp.int32)
    smem = pl.BlockSpec(memory_space=pltpu.SMEM)
    vmem = pl.BlockSpec(memory_space=pltpu.VMEM)

    rows = query_weight.shape[0] // 4
    weight = pl.pallas_call(
        slice_kernel,
        out_shape=jax.ShapeDtypeStruct((16, rows, 3 * HD), jnp.bfloat16),
        in_specs=[smem] + [vmem] * 3,
        out_specs=vmem,
        name="slice",
    )(where, key_weight, value_weight, query_weight)
    weight = lax.all_to_all(weight, "z", 0, 0, tiled=True)

    cut = count // 2
    before, after = shifted(own, "x", 1), shifted(own, "x", -1)
    weight, before, after = lax.optimization_barrier((weight, before, after))
    weight = spread(weight, ("yh", "yl")).reshape(2, 2, 16, rows, 3 * HD)
    partner = [shifted(part, "core", 1) for part in weight]
    low_far, high_far = shifted(before[:cut], "x", 1), shifted(after[cut:], "x", -1)
    token_sets = (own, before, after, low_far, high_far)
    grads = cotangent[0].reshape(count, HEADS, HD).transpose(1, 0, 2)
    grads = lax.all_to_all(grads, "x", 0, 0, tiled=True)

    queries, kv = project(where, weight, *partner, token_sets)
    across = shifted(kv, "yh", 1)
    across, grads = lax.optimization_barrier((across, grads))
    pieces = [kv, shifted(kv, "core", 1), across, shifted(across, "core", 1)]

    attended, partial = attention(
        where, rand_owner[0], rand_offset[0], global_ids, grads, queries, pieces, token_sets
    )
    returned = [attended[0]] + [shifted(attended[s], "x", -s) for s in range(1, HEADS)]
    partial = lax.all_to_all(partial, ("yh", "yl", "core"), 0, 0, tiled=True)
    partial = jnp.sum(partial.astype(jnp.float32), axis=0).astype(jnp.bfloat16)
    partial, returned[1], returned[3] = lax.optimization_barrier(
        (partial, returned[1], returned[3])
    )
    partial = lax.all_to_all(partial, "z", 0, 0, tiled=True)
    partial = jnp.sum(partial.astype(jnp.float32), axis=0)
    partial, returned[2] = lax.optimization_barrier((partial, returned[2]))
    attn = pl.pallas_call(
        merge_kernel,
        out_shape=jax.ShapeDtypeStruct((count, HEADS * HD), jnp.bfloat16),
        in_specs=[smem] + [vmem] * HEADS,
        out_specs=vmem,
        name="merge",
    )(where, *returned)

    final = spread(partial, ("yh", "x", "core")).reshape(2, 4, 2, rows, HD)
    query_grad = final.transpose(0, 2, 3, 1, 4).reshape(4 * rows, HEADS * HD)
    return attn[None], query_grad


def solution(mesh):
    fine = Mesh(
        mesh.devices.reshape(2, 4, 2, 16, 2),
        ("yh", "x", "core", "z", "yl"),
        axis_types=(jax.sharding.AxisType.Auto,) * 5,
    )
    ctx, fsdp = ("yh", "x", "core"), ("z", "yl")
    placed = (
        P(fsdp, ctx, None),
        P(fsdp, None),
        P(fsdp, None),
        P(fsdp, None),
        P(fsdp, ctx, None),
        P(fsdp, None, None),
        P(fsdp, None, None),
        P(fsdp, None),
    )
    return jax.shard_map(
        per_device,
        mesh=fine,
        in_specs=placed,
        out_specs=(P(fsdp, ctx, None), P(fsdp, None)),
        check_vma=False,
    )
```

```python
import jax
import jax.numpy as jnp
from jax import lax
from jax.experimental import pallas as pl
from jax.experimental.pallas import tpu as pltpu
from jax.sharding import Mesh
from jax.sharding import PartitionSpec as P

HD = 128
BLK = 64
RND = 3
GLB = 2
NBL = 4
PIECE_BLOCKS = 16
PIECES = 4
HEADS = 4
MASKED = -1e30

NT = (((1,), (1,)), ((), ()))
NN = (((1,), (0,)), ((), ()))
TN = (((0,), (0,)), ((), ()))


def dot32(a, b, dims):
    return lax.dot_general(a, b, dims, preferred_element_type=jnp.float32)


def spread(block, axes):
    count = lax.axis_size(axes)
    return lax.all_to_all(
        jnp.broadcast_to(block[None], (count, *block.shape)), axes, 0, 0, tiled=True
    )


def shifted(block, axis, step):
    count = lax.axis_size(axis)
    return lax.ppermute(block, axis, [(i, (i + step) % count) for i in range(count)])


def slice_kernel(where_ref, key_ref, value_ref, query_ref, out_ref):
    count, rows, _ = out_ref.shape
    start = pl.multiple_of((where_ref[0] * 2 + where_ref[2]) * rows, rows)
    col = pl.multiple_of(where_ref[1] * HD, HD)
    for i, ref in enumerate((key_ref, value_ref, query_ref)):
        part = ref[pl.ds(start, rows), pl.ds(col, HD)]
        for copy in range(count):
            out_ref[copy, :, i * HD : (i + 1) * HD] = part


def project_kernel(where_ref, mine_ref, theirs_a_ref, theirs_b_ref, *rest):
    theirs = (theirs_a_ref, theirs_b_ref)
    token_refs, (q_ref, kv_ref, w_ref) = rest[:-3], rest[-3:]
    core = where_ref[2]
    _, _, depth, rows, width = mine_ref.shape

    def assemble(z, carry):
        for yl in range(2):
            for yh in range(2):
                base = (z * 2 + yl) * 4 * rows + yh * 2 * rows
                here = pl.multiple_of(base + core * rows, rows)
                there = pl.multiple_of(base + (1 - core) * rows, rows)
                w_ref[pl.ds(here, rows), :] = mine_ref[yh, yl, z]
                w_ref[pl.ds(there, rows), :] = theirs[yh][yl, z]
        return carry

    lax.fori_loop(0, depth, assemble, 0)
    for slot, group in token_groups(token_refs):
        tokens = jnp.concatenate([ref[...] for ref in group], axis=0)
        size = tokens.shape[0]
        out = dot32(tokens, w_ref[...], NN).astype(jnp.bfloat16)
        kv_ref[slot * NBL : (slot + 1) * NBL] = out[:, : 2 * HD].reshape(NBL, BLK, 2 * HD)
        q_ref[slot * size : (slot + 1) * size, :] = out[:, 2 * HD :]


def token_groups(refs):
    own, before, after, low_far, high_far = refs
    return [(0, (own,)), (1, (before,)), (3, (after,)), (2, (low_far, high_far))]


def project(where, mine, theirs_a, theirs_b, token_sets):
    count, depth = token_sets[0].shape
    total = count * HEADS
    vmem = pl.BlockSpec(memory_space=pltpu.VMEM)
    return pl.pallas_call(
        project_kernel,
        out_shape=(
            jax.ShapeDtypeStruct((total, HD), jnp.bfloat16),
            jax.ShapeDtypeStruct((PIECE_BLOCKS, BLK, 2 * HD), jnp.bfloat16),
        ),
        in_specs=[pl.BlockSpec(memory_space=pltpu.SMEM)] + [vmem] * (3 + len(token_sets)),
        out_specs=(vmem, vmem),
        scratch_shapes=[pltpu.VMEM((depth, 3 * HD), jnp.bfloat16)],
        compiler_params=pltpu.CompilerParams(vmem_limit_bytes=24 * 1024 * 1024),
        name="project",
    )(where, mine, theirs_a, theirs_b, *token_sets)


def attention_kernel(where_ref, owner_ref, offset_ref, global_ref, *rest):
    given, pieces, token_refs = rest[:2], rest[2 : 2 + PIECES], rest[2 + PIECES : -9]
    keep_ref, send_ref, part_ref, kv_ref, g_ref, q_ref, gq_ref, t_ref, sems = rest[-9:]
    pairs = [
        (piece, kv_ref.at[pl.ds(slot * PIECE_BLOCKS, PIECE_BLOCKS)])
        for slot, piece in enumerate(pieces)
    ]
    pairs += list(zip(given, (g_ref, q_ref)))
    first = len(pairs)
    for slot, group in token_groups(token_refs):
        size = group[0].shape[0]
        pairs += [
            (ref, t_ref.at[slot, pl.ds(i * size, size)]) for i, ref in enumerate(group)
        ]
    copies = [
        pltpu.make_async_copy(source, target, sems.at[i])
        for i, (source, target) in enumerate(pairs)
    ]
    copies, later = copies[:first], copies[first:]
    for copy in copies:
        copy.start()
    my_yh, my_x, my_core = where_ref[0], where_ref[1], where_ref[2]

    def place(block):
        shard, inside = block // NBL, lax.rem(block, NBL)
        yh, x, core = shard // 8, lax.rem(shard // 2, 4), lax.rem(shard, 2)
        piece = jnp.where(core == my_core, 0, 1) + jnp.where(yh == my_yh, 0, 2)
        slot = lax.rem(my_x + 4 - x, 4)
        return piece * PIECE_BLOCKS + slot * NBL + inside

    for copy in copies:
        copy.wait()
    for copy in later:
        copy.start()

    lane = lax.broadcasted_iota(jnp.int32, (1, 2 * BLK), 1)
    total = PIECES * PIECE_BLOCKS
    scale = HD**-0.5
    odd = lax.rem(my_x, 2)

    def step(inside, carry):
        rows = pl.ds(pl.multiple_of(inside * BLK, BLK), BLK)
        ks, vs, ss, gps = [], [], [], []
        for slot in range(HEADS):
            x = lax.rem(my_x + 4 - slot, 4)
            block = ((my_yh * 4 + x) * 2 + my_core) * NBL + inside
            left = jnp.maximum(block - 1, 0)
            right = jnp.minimum(block + 1, total - 1)
            named = [left, right, block]
            for r in range(RND):
                named.append(owner_ref[block, r] * NBL + offset_ref[block, r])
            for r in range(GLB):
                named.append(global_ref[0, r])
            kv = jnp.concatenate([kv_ref[place(b)] for b in named], axis=0)
            k, v = kv[:, :HD], kv[:, HD:]
            allowed = ((lane < BLK) & (block > 0)) | ((lane >= BLK) & (block < total - 1))
            place_rows = pl.ds(pl.multiple_of(slot * NBL * BLK + inside * BLK, BLK), BLK)
            s = dot32(q_ref[place_rows, :], k, NT) * scale
            s = jnp.concatenate(
                [jnp.where(allowed, s[:, : 2 * BLK], MASKED), s[:, 2 * BLK :]], axis=1
            )
            ks.append(k)
            vs.append(v)
            ss.append(s)
            gps.append(dot32(g_ref[x, rows, :], v, NT))
        for slot in range(HEADS):
            s, gp = ss[slot], gps[slot]
            e = jnp.exp(s - jnp.max(s, axis=1, keepdims=True))
            p = e * (1.0 / jnp.sum(e, axis=1, keepdims=True))
            delta = jnp.sum(p * gp, axis=1, keepdims=True)
            ds = (p * (gp - delta) * scale).astype(jnp.bfloat16)
            out = dot32(p.astype(jnp.bfloat16), vs[slot], NN).astype(jnp.bfloat16)
            if slot % 2 == 0:
                keep_ref[slot // 2, rows, :] = out
            else:
                near = 1 - odd if slot == 1 else odd
                send_ref[near, rows, :] = out
            gq_ref[slot, rows, :] = dot32(ds, ks[slot], NN).astype(jnp.bfloat16)
        return carry

    lax.fori_loop(0, NBL, step, 0)

    acc = None
    for copy in later:
        copy.wait()
    for slot in range(HEADS):
        term = dot32(gq_ref[slot], t_ref[slot], TN)
        acc = term if acc is None else acc + term
    rows = part_ref.shape[2]
    for z in range(16):
        turned = acc[:, z * HD : (z + 1) * HD].T.astype(jnp.bfloat16)
        for yl in range(2):
            for q in range(4):
                at = yl * 4 * rows + q * rows
                part_ref[((q // 2) * 2 + yl) * 2 + q % 2, z] = turned[at : at + rows]


def attention(where, owners, offsets, global_list, grads, queries, pieces, token_sets):
    smem = pl.BlockSpec(memory_space=pltpu.SMEM)
    vmem = pl.BlockSpec(memory_space=pltpu.VMEM)
    return pl.pallas_call(
        attention_kernel,
        out_shape=(
            jax.ShapeDtypeStruct((2, *grads.shape[1:]), jnp.bfloat16),
            jax.ShapeDtypeStruct((2, *grads.shape[1:]), jnp.bfloat16),
            jax.ShapeDtypeStruct((8, 16, 16, HD), jnp.bfloat16),
        ),
        in_specs=[smem] * 4
        + [pl.BlockSpec(memory_space=pl.ANY)] * (2 + PIECES + len(token_sets)),
        out_specs=(vmem,) * 3,
        scratch_shapes=[
            pltpu.VMEM((PIECES * PIECE_BLOCKS, BLK, 2 * HD), jnp.bfloat16),
            pltpu.VMEM(grads.shape, jnp.bfloat16),
            pltpu.VMEM(queries.shape, jnp.bfloat16),
            pltpu.VMEM(grads.shape, jnp.bfloat16),
            pltpu.VMEM((HEADS, *token_sets[0].shape), jnp.bfloat16),
            pltpu.SemaphoreType.DMA((2 + PIECES + len(token_sets),)),
        ],
        compiler_params=pltpu.CompilerParams(vmem_limit_bytes=56 * 1024 * 1024),
        name="attention",
    )(where, owners, offsets, global_list, grads, queries, *pieces, *token_sets)


def merge_kernel(where_ref, keep_ref, next_ref, far_ref, out_ref):
    x = where_ref[1]
    odd, high = lax.rem(x, 2), x // 2
    parts = (keep_ref.at[0], next_ref.at[0], far_ref.at[0], far_ref.at[1])
    for flip, ref in enumerate(parts):
        low = odd if flip % 2 == 0 else 1 - odd
        top = high if flip < 2 else 1 - high
        head = top * 2 + low
        out_ref[:, pl.ds(pl.multiple_of(head * HD, HD), HD)] = ref[...]


def exchanged(block, flip):
    return lax.ppermute(block, "x", [(i, i ^ flip) for i in range(HEADS)])


def per_device(
    tokens, query_weight, key_weight, value_weight, cotangent, rand_owner, rand_offset, global_ids
):
    own = tokens[0]
    count, depth = own.shape
    where = jnp.stack(
        [lax.axis_index("yh"), lax.axis_index("x"), lax.axis_index("core")]
    ).astype(jnp.int32)
    smem = pl.BlockSpec(memory_space=pltpu.SMEM)
    vmem = pl.BlockSpec(memory_space=pltpu.VMEM)

    rows = query_weight.shape[0] // 4
    weight = pl.pallas_call(
        slice_kernel,
        out_shape=jax.ShapeDtypeStruct((16, rows, 3 * HD), jnp.bfloat16),
        in_specs=[smem] + [vmem] * 3,
        out_specs=vmem,
        name="slice",
    )(where, key_weight, value_weight, query_weight)
    weight = lax.all_to_all(weight, "z", 0, 0, tiled=True)

    cut = count // 2
    before, after = shifted(own, "x", 1), shifted(own, "x", -1)
    weight, before, after = lax.optimization_barrier((weight, before, after))
    weight = spread(weight, ("yh", "yl")).reshape(2, 2, 16, rows, 3 * HD)
    partner = [shifted(part, "core", 1) for part in weight]
    low_far, high_far = shifted(before[:cut], "x", 1), shifted(after[cut:], "x", -1)
    token_sets = (own, before, after, low_far, high_far)
    grads = cotangent[0].reshape(count, HEADS, HD).transpose(1, 0, 2)
    grads = lax.all_to_all(grads, "x", 0, 0, tiled=True)

    queries, kv = project(where, weight, *partner, token_sets)
    across = shifted(kv, "yh", 1)
    across, grads = lax.optimization_barrier((across, grads))
    pieces = [kv, shifted(kv, "core", 1), across, shifted(across, "core", 1)]

    kept, sent, partial = attention(
        where, rand_owner[0], rand_offset[0], global_ids, grads, queries, pieces, token_sets
    )
    from_next = exchanged(sent, 1)
    partial = lax.all_to_all(partial, ("yh", "yl", "core"), 0, 0, tiled=True)
    partial = jnp.sum(partial.astype(jnp.float32), axis=0).astype(jnp.bfloat16)
    partial, from_next = lax.optimization_barrier((partial, from_next))
    from_far = exchanged(jnp.stack([kept[1], from_next[1]]), 2)
    partial = lax.all_to_all(partial, "z", 0, 0, tiled=True)
    partial = jnp.sum(partial.astype(jnp.float32), axis=0)
    partial, from_far = lax.optimization_barrier((partial, from_far))
    attn = pl.pallas_call(
        merge_kernel,
        out_shape=jax.ShapeDtypeStruct((count, HEADS * HD), jnp.bfloat16),
        in_specs=[smem] + [vmem] * 3,
        out_specs=vmem,
        name="merge",
    )(where, kept, from_next, from_far)

    final = spread(partial, ("yh", "x", "core")).reshape(2, 4, 2, rows, HD)
    query_grad = final.transpose(0, 2, 3, 1, 4).reshape(4 * rows, HEADS * HD)
    return attn[None], query_grad


def solution(mesh):
    fine = Mesh(
        mesh.devices.reshape(2, 4, 2, 16, 2),
        ("yh", "x", "core", "z", "yl"),
        axis_types=(jax.sharding.AxisType.Auto,) * 5,
    )
    ctx, fsdp = ("yh", "x", "core"), ("z", "yl")
    placed = (
        P(fsdp, ctx, None),
        P(fsdp, None),
        P(fsdp, None),
        P(fsdp, None),
        P(fsdp, ctx, None),
        P(fsdp, None, None),
        P(fsdp, None, None),
        P(fsdp, None),
    )
    return jax.shard_map(
        per_device,
        mesh=fine,
        in_specs=placed,
        out_specs=(P(fsdp, ctx, None), P(fsdp, None)),
        check_vma=False,
    )
```

```python
import functools

import jax
import jax.numpy as jnp
from jax import lax
from jax.experimental import pallas as pl
from jax.experimental.pallas import tpu as pltpu
from jax.sharding import Mesh
from jax.sharding import PartitionSpec as P

HD = 128
BLK = 64
RND = 3
GLB = 2
NBL = 4
PIECE_BLOCKS = 16
PIECES = 4
HEADS = 4
MASKED = -1e30

NT = (((1,), (1,)), ((), ()))
NN = (((1,), (0,)), ((), ()))
TN = (((0,), (0,)), ((), ()))


def dot32(a, b, dims):
    return lax.dot_general(a, b, dims, preferred_element_type=jnp.float32)


def spread(block, axes):
    count = lax.axis_size(axes)
    return lax.all_to_all(
        jnp.broadcast_to(block[None], (count, *block.shape)), axes, 0, 0, tiled=True
    )


def shifted(block, axis, step):
    count = lax.axis_size(axis)
    return lax.ppermute(block, axis, [(i, (i + step) % count) for i in range(count)])


def slice_kernel(where_ref, key_ref, value_ref, query_ref, grad_ref, out_ref, *grad_outs):
    for hop, ref in enumerate(grad_outs):
        head = lax.rem(where_ref[1] + hop, HEADS)
        ref[...] = grad_ref[:, pl.ds(pl.multiple_of(head * HD, HD), HD)]
    count, rows, _ = out_ref.shape
    start = pl.multiple_of((where_ref[0] * 2 + where_ref[2]) * rows, rows)
    col = pl.multiple_of(where_ref[1] * HD, HD)
    for i, ref in enumerate((key_ref, value_ref, query_ref)):
        part = ref[pl.ds(start, rows), pl.ds(col, HD)]
        for copy in range(count):
            out_ref[copy, :, i * HD : (i + 1) * HD] = part


def project_kernel(cols, where_ref, mine_ref, theirs_a_ref, theirs_b_ref, *rest):
    theirs = (theirs_a_ref, theirs_b_ref)
    token_refs, (out_ref, w_ref) = rest[:-2], rest[-2:]
    core = where_ref[2]
    _, _, depth, rows, width = mine_ref.shape

    def assemble(z, carry):
        for yl in range(2):
            for yh in range(2):
                base = (z * 2 + yl) * 4 * rows + yh * 2 * rows
                here = pl.multiple_of(base + core * rows, rows)
                there = pl.multiple_of(base + (1 - core) * rows, rows)
                w_ref[pl.ds(here, rows), :] = mine_ref[yh, yl, z, :, cols]
                w_ref[pl.ds(there, rows), :] = theirs[yh][yl, z, :, cols]
        return carry

    lax.fori_loop(0, depth, assemble, 0)
    for slot, group in token_groups(token_refs):
        tokens = jnp.concatenate([ref[...] for ref in group], axis=0)
        size = tokens.shape[0]
        out = dot32(tokens, w_ref[...], NN).astype(jnp.bfloat16)
        out_ref[slot * size : (slot + 1) * size, :] = out


def token_groups(refs):
    own, before, after, low_far, high_far = refs
    return [(0, (own,)), (1, (before,)), (3, (after,)), (2, (low_far, high_far))]


def project(name, cols, where, mine, theirs_a, theirs_b, token_sets):
    count, depth = token_sets[0].shape
    total, width = count * HEADS, cols.stop - cols.start
    vmem = pl.BlockSpec(memory_space=pltpu.VMEM)
    return pl.pallas_call(
        functools.partial(project_kernel, cols),
        out_shape=jax.ShapeDtypeStruct((total, width), jnp.bfloat16),
        in_specs=[pl.BlockSpec(memory_space=pltpu.SMEM)] + [vmem] * (3 + len(token_sets)),
        out_specs=vmem,
        scratch_shapes=[pltpu.VMEM((depth, width), jnp.bfloat16)],
        compiler_params=pltpu.CompilerParams(vmem_limit_bytes=24 * 1024 * 1024),
        cost_estimate=pl.CostEstimate(
            flops=2 * total * depth * width,
            bytes_accessed=2 * depth * (total + width),
            transcendentals=0,
        ),
        name=name,
    )(where, mine, theirs_a, theirs_b, *token_sets)


def attention_kernel(where_ref, owner_ref, offset_ref, global_ref, *rest):
    given, pieces = rest[: 1 + HEADS], rest[1 + HEADS : 1 + HEADS + PIECES]
    token_refs = rest[1 + HEADS + PIECES : -9]
    keep_ref, send_ref, part_ref, kv_ref, g_ref, q_ref, gq_ref, t_ref, sems = rest[-9:]
    pairs = [
        (piece, kv_ref.at[pl.ds(slot * PIECE_BLOCKS, PIECE_BLOCKS)])
        for slot, piece in enumerate(pieces)
    ]
    pairs += [(ref, g_ref.at[slot]) for slot, ref in enumerate(given[:-1])]
    pairs.append((given[-1], q_ref))
    first = len(pairs)
    for slot, group in token_groups(token_refs):
        size = group[0].shape[0]
        pairs += [
            (ref, t_ref.at[slot, pl.ds(i * size, size)]) for i, ref in enumerate(group)
        ]
    copies = [
        pltpu.make_async_copy(source, target, sems.at[i])
        for i, (source, target) in enumerate(pairs)
    ]
    copies, later = copies[:first], copies[first:]
    for copy in copies:
        copy.start()
    my_yh, my_x, my_core = where_ref[0], where_ref[1], where_ref[2]

    def place(block):
        shard, inside = block // NBL, lax.rem(block, NBL)
        yh, x, core = shard // 8, lax.rem(shard // 2, 4), lax.rem(shard, 2)
        piece = jnp.where(core == my_core, 0, 1) + jnp.where(yh == my_yh, 0, 2)
        slot = lax.rem(my_x + 4 - x, 4)
        return piece * PIECE_BLOCKS + slot * NBL + inside

    for copy in copies:
        copy.wait()
    for copy in later:
        copy.start()

    lane = lax.broadcasted_iota(jnp.int32, (1, 2 * BLK), 1)
    total = PIECES * PIECE_BLOCKS
    scale = HD**-0.5
    odd = lax.rem(my_x, 2)

    def step(inside, carry):
        rows = pl.ds(pl.multiple_of(inside * BLK, BLK), BLK)
        ks, vs, ss, gps = [], [], [], []
        for slot in range(HEADS):
            x = lax.rem(my_x + 4 - slot, 4)
            block = ((my_yh * 4 + x) * 2 + my_core) * NBL + inside
            left = jnp.maximum(block - 1, 0)
            right = jnp.minimum(block + 1, total - 1)
            named = [left, right, block]
            for r in range(RND):
                named.append(owner_ref[block, r] * NBL + offset_ref[block, r])
            for r in range(GLB):
                named.append(global_ref[0, r])
            kv = jnp.concatenate([kv_ref[place(b)] for b in named], axis=0)
            k, v = kv[:, :HD], kv[:, HD:]
            allowed = ((lane < BLK) & (block > 0)) | ((lane >= BLK) & (block < total - 1))
            place_rows = pl.ds(pl.multiple_of(slot * NBL * BLK + inside * BLK, BLK), BLK)
            s = dot32(q_ref[place_rows, :], k, NT) * scale
            s = jnp.concatenate(
                [jnp.where(allowed, s[:, : 2 * BLK], MASKED), s[:, 2 * BLK :]], axis=1
            )
            ks.append(k)
            vs.append(v)
            ss.append(s)
            gps.append(dot32(g_ref[slot, rows, :], v, NT))
        for slot in range(HEADS):
            s, gp = ss[slot], gps[slot]
            e = jnp.exp(s - jnp.max(s, axis=1, keepdims=True))
            p = e * (1.0 / jnp.sum(e, axis=1, keepdims=True))
            delta = jnp.sum(p * gp, axis=1, keepdims=True)
            ds = (p * (gp - delta) * scale).astype(jnp.bfloat16)
            out = dot32(p.astype(jnp.bfloat16), vs[slot], NN).astype(jnp.bfloat16)
            if slot % 2 == 0:
                keep_ref[slot // 2, rows, :] = out
            else:
                near = 1 - odd if slot == 1 else odd
                send_ref[near, rows, :] = out
            gq_ref[slot, rows, :] = dot32(ds, ks[slot], NN).astype(jnp.bfloat16)
        return carry

    lax.fori_loop(0, NBL, step, 0)

    acc = None
    for copy in later:
        copy.wait()
    for slot in range(HEADS):
        term = dot32(gq_ref[slot], t_ref[slot], TN)
        acc = term if acc is None else acc + term
    rows = part_ref.shape[2]
    for z in range(16):
        turned = acc[:, z * HD : (z + 1) * HD].T.astype(jnp.bfloat16)
        for yl in range(2):
            for q in range(4):
                at = yl * 4 * rows + q * rows
                part_ref[((q // 2) * 2 + yl) * 2 + q % 2, z] = turned[at : at + rows]


def attention(where, owners, offsets, global_list, grads, queries, pieces, token_sets):
    smem = pl.BlockSpec(memory_space=pltpu.SMEM)
    vmem = pl.BlockSpec(memory_space=pltpu.VMEM)
    return pl.pallas_call(
        attention_kernel,
        out_shape=(
            jax.ShapeDtypeStruct((2, *grads[0].shape), jnp.bfloat16),
            jax.ShapeDtypeStruct((2, *grads[0].shape), jnp.bfloat16),
            jax.ShapeDtypeStruct((8, 16, 16, HD), jnp.bfloat16),
        ),
        in_specs=[smem] * 4
        + [pl.BlockSpec(memory_space=pl.ANY)] * (1 + HEADS + PIECES + len(token_sets)),
        out_specs=(vmem,) * 3,
        scratch_shapes=[
            pltpu.VMEM((PIECES * PIECE_BLOCKS, BLK, 2 * HD), jnp.bfloat16),
            pltpu.VMEM((HEADS, *grads[0].shape), jnp.bfloat16),
            pltpu.VMEM(queries.shape, jnp.bfloat16),
            pltpu.VMEM((HEADS, *grads[0].shape), jnp.bfloat16),
            pltpu.VMEM((HEADS, *token_sets[0].shape), jnp.bfloat16),
            pltpu.SemaphoreType.DMA((1 + HEADS + PIECES + len(token_sets),)),
        ],
        compiler_params=pltpu.CompilerParams(vmem_limit_bytes=56 * 1024 * 1024),
        name="attention",
    )(where, owners, offsets, global_list, *grads, queries, *pieces, *token_sets)


def merge_kernel(where_ref, keep_ref, next_ref, far_ref, out_ref):
    x = where_ref[1]
    odd, high = lax.rem(x, 2), x // 2
    parts = (keep_ref.at[0], next_ref.at[0], far_ref.at[0], far_ref.at[1])
    for flip, ref in enumerate(parts):
        low = odd if flip % 2 == 0 else 1 - odd
        top = high if flip < 2 else 1 - high
        head = top * 2 + low
        out_ref[:, pl.ds(pl.multiple_of(head * HD, HD), HD)] = ref[...]


def exchanged(block, flip):
    return lax.ppermute(block, "x", [(i, i ^ flip) for i in range(HEADS)])


def per_device(
    tokens, query_weight, key_weight, value_weight, cotangent, rand_owner, rand_offset, global_ids
):
    own = tokens[0]
    count, depth = own.shape
    where = jnp.stack(
        [lax.axis_index("yh"), lax.axis_index("x"), lax.axis_index("core")]
    ).astype(jnp.int32)
    smem = pl.BlockSpec(memory_space=pltpu.SMEM)
    vmem = pl.BlockSpec(memory_space=pltpu.VMEM)

    rows = query_weight.shape[0] // 4
    weight, *grads = pl.pallas_call(
        slice_kernel,
        out_shape=(jax.ShapeDtypeStruct((16, rows, 3 * HD), jnp.bfloat16),)
        + (jax.ShapeDtypeStruct((count, HD), jnp.bfloat16),) * HEADS,
        in_specs=[smem] + [vmem] * 4,
        out_specs=(vmem,) * (1 + HEADS),
        name="slice",
    )(where, key_weight, value_weight, query_weight, cotangent[0])
    weight = lax.all_to_all(weight, "z", 0, 0, tiled=True)

    cut = count // 2
    before, after = shifted(own, "x", 1), shifted(own, "x", -1)
    grads = [grads[0]] + [shifted(grads[h], "x", h) for h in range(1, HEADS)]
    weight, before, after, low_next, high_next, grads = lax.optimization_barrier(
        (weight, before, after, before[:cut], after[cut:], grads)
    )
    weight = spread(weight, ("yh", "yl")).reshape(2, 2, 16, rows, 3 * HD)
    partner = [shifted(part, "core", 1) for part in weight]
    low_far, high_far = shifted(low_next, "x", 1), shifted(high_next, "x", -1)
    token_sets = (own, before, after, low_far, high_far)
    kv = project(
        "keys_values", slice(0, 2 * HD), where, weight, *partner, token_sets
    ).reshape(PIECE_BLOCKS, BLK, 2 * HD)
    queries = project(
        "queries", slice(2 * HD, 3 * HD), where, weight, *partner, token_sets
    )
    across = shifted(kv, "yh", 1)
    across, queries = lax.optimization_barrier((across, queries))
    pieces = [kv, shifted(kv, "core", 1), across, shifted(across, "core", 1)]

    kept, sent, partial = attention(
        where, rand_owner[0], rand_offset[0], global_ids, grads, queries, pieces, token_sets
    )
    from_next = exchanged(sent, 1)
    partial = lax.all_to_all(partial, ("yh", "yl", "core"), 0, 0, tiled=True)
    partial = jnp.sum(partial.astype(jnp.float32), axis=0).astype(jnp.bfloat16)
    partial, from_next = lax.optimization_barrier((partial, from_next))
    from_far = exchanged(jnp.stack([kept[1], from_next[1]]), 2)
    partial = lax.all_to_all(partial, "z", 0, 0, tiled=True)
    partial = jnp.sum(partial.astype(jnp.float32), axis=0)
    partial, from_far = lax.optimization_barrier((partial, from_far))
    attn = pl.pallas_call(
        merge_kernel,
        out_shape=jax.ShapeDtypeStruct((count, HEADS * HD), jnp.bfloat16),
        in_specs=[smem] + [vmem] * 3,
        out_specs=vmem,
        name="merge",
    )(where, kept, from_next, from_far)

    final = spread(partial, ("yh", "x", "core")).reshape(2, 4, 2, rows, HD)
    query_grad = final.transpose(0, 2, 3, 1, 4).reshape(4 * rows, HEADS * HD)
    return attn[None], query_grad


def solution(mesh):
    fine = Mesh(
        mesh.devices.reshape(2, 4, 2, 16, 2),
        ("yh", "x", "core", "z", "yl"),
        axis_types=(jax.sharding.AxisType.Auto,) * 5,
    )
    ctx, fsdp = ("yh", "x", "core"), ("z", "yl")
    placed = (
        P(fsdp, ctx, None),
        P(fsdp, None),
        P(fsdp, None),
        P(fsdp, None),
        P(fsdp, ctx, None),
        P(fsdp, None, None),
        P(fsdp, None, None),
        P(fsdp, None),
    )
    return jax.shard_map(
        per_device,
        mesh=fine,
        in_specs=placed,
        out_specs=(P(fsdp, ctx, None), P(fsdp, None)),
        check_vma=False,
    )
```

```python
import functools

import jax
import jax.numpy as jnp
from jax import lax
from jax.experimental import pallas as pl
from jax.experimental.pallas import tpu as pltpu
from jax.sharding import Mesh
from jax.sharding import PartitionSpec as P

HD = 128
BLK = 64
RND = 3
GLB = 2
NBL = 4
PIECE_BLOCKS = 16
PIECES = 4
HEADS = 4
MASKED = -1e30

NT = (((1,), (1,)), ((), ()))
NN = (((1,), (0,)), ((), ()))
TN = (((0,), (0,)), ((), ()))


def dot32(a, b, dims):
    return lax.dot_general(a, b, dims, preferred_element_type=jnp.float32)


def spread(block, axes):
    count = lax.axis_size(axes)
    return lax.all_to_all(
        jnp.broadcast_to(block[None], (count, *block.shape)), axes, 0, 0, tiled=True
    )


def shifted(block, axis, step):
    count = lax.axis_size(axis)
    return lax.ppermute(block, axis, [(i, (i + step) % count) for i in range(count)])


def slice_kernel(where_ref, key_ref, value_ref, query_ref, grad_ref, out_ref, *grad_outs):
    for hop, ref in enumerate(grad_outs):
        head = lax.rem(where_ref[1] + hop, HEADS)
        ref[...] = grad_ref[:, pl.ds(pl.multiple_of(head * HD, HD), HD)]
    count, rows, _ = out_ref.shape
    start = pl.multiple_of((where_ref[0] * 2 + where_ref[2]) * rows, rows)
    col = pl.multiple_of(where_ref[1] * HD, HD)
    for i, ref in enumerate((key_ref, value_ref, query_ref)):
        part = ref[pl.ds(start, rows), pl.ds(col, HD)]
        for copy in range(count):
            out_ref[copy, :, i * HD : (i + 1) * HD] = part


def project_kernel(cols, where_ref, mine_ref, theirs_a_ref, theirs_b_ref, *rest):
    theirs = (theirs_a_ref, theirs_b_ref)
    token_refs, (out_ref, w_ref) = rest[:-2], rest[-2:]
    core = where_ref[2]
    _, _, depth, rows, width = mine_ref.shape

    def assemble(z, carry):
        for yl in range(2):
            for yh in range(2):
                base = (z * 2 + yl) * 4 * rows + yh * 2 * rows
                here = pl.multiple_of(base + core * rows, rows)
                there = pl.multiple_of(base + (1 - core) * rows, rows)
                w_ref[pl.ds(here, rows), :] = mine_ref[yh, yl, z, :, cols]
                w_ref[pl.ds(there, rows), :] = theirs[yh][yl, z, :, cols]
        return carry

    lax.fori_loop(0, depth, assemble, 0)
    for slot, group in token_groups(token_refs):
        tokens = jnp.concatenate([ref[...] for ref in group], axis=0)
        size = tokens.shape[0]
        out = dot32(tokens, w_ref[...], NN).astype(jnp.bfloat16)
        out_ref[slot * size : (slot + 1) * size, :] = out


def token_groups(refs):
    own, before, after, low_far, high_far = refs
    return [(0, (own,)), (1, (before,)), (3, (after,)), (2, (low_far, high_far))]


def project(name, cols, where, mine, theirs_a, theirs_b, token_sets):
    count, depth = token_sets[0].shape
    total, width = count * HEADS, cols.stop - cols.start
    vmem = pl.BlockSpec(memory_space=pltpu.VMEM)
    return pl.pallas_call(
        functools.partial(project_kernel, cols),
        out_shape=jax.ShapeDtypeStruct((total, width), jnp.bfloat16),
        in_specs=[pl.BlockSpec(memory_space=pltpu.SMEM)] + [vmem] * (3 + len(token_sets)),
        out_specs=vmem,
        scratch_shapes=[pltpu.VMEM((depth, width), jnp.bfloat16)],
        compiler_params=pltpu.CompilerParams(vmem_limit_bytes=24 * 1024 * 1024),
        cost_estimate=pl.CostEstimate(
            flops=2 * total * depth * width,
            bytes_accessed=2 * depth * (total + width),
            transcendentals=0,
        ),
        name=name,
    )(where, mine, theirs_a, theirs_b, *token_sets)


def attention_kernel(where_ref, owner_ref, offset_ref, global_ref, *rest):
    given, pieces = rest[: 1 + HEADS], rest[1 + HEADS : 1 + HEADS + PIECES]
    token_refs = rest[1 + HEADS + PIECES : -9]
    keep_ref, send_ref, part_ref, kv_ref, g_ref, q_ref, gq_ref, t_ref, sems = rest[-9:]
    pairs = [
        (piece, kv_ref.at[pl.ds(slot * PIECE_BLOCKS, PIECE_BLOCKS)])
        for slot, piece in enumerate(pieces)
    ]
    pairs += [(ref, g_ref.at[slot]) for slot, ref in enumerate(given[:-1])]
    pairs.append((given[-1], q_ref))
    first = len(pairs)
    for slot, group in token_groups(token_refs):
        size = group[0].shape[0]
        pairs += [
            (ref, t_ref.at[slot, pl.ds(i * size, size)]) for i, ref in enumerate(group)
        ]
    copies = [
        pltpu.make_async_copy(source, target, sems.at[i])
        for i, (source, target) in enumerate(pairs)
    ]
    copies, later = copies[:first], copies[first:]
    for copy in copies:
        copy.start()
    my_yh, my_x, my_core = where_ref[0], where_ref[1], where_ref[2]

    def place(block):
        shard, inside = block // NBL, lax.rem(block, NBL)
        yh, x, core = shard // 8, lax.rem(shard // 2, 4), lax.rem(shard, 2)
        piece = jnp.where(core == my_core, 0, 1) + jnp.where(yh == my_yh, 0, 2)
        slot = lax.rem(my_x + 4 - x, 4)
        return piece * PIECE_BLOCKS + slot * NBL + inside

    for copy in copies:
        copy.wait()
    for copy in later:
        copy.start()

    lane = lax.broadcasted_iota(jnp.int32, (1, 2 * BLK), 1)
    total = PIECES * PIECE_BLOCKS
    scale = HD**-0.5
    odd = lax.rem(my_x, 2)

    def step(inside, carry):
        rows = pl.ds(pl.multiple_of(inside * BLK, BLK), BLK)
        ks, vs, ss, gps = [], [], [], []
        for slot in range(HEADS):
            x = lax.rem(my_x + 4 - slot, 4)
            block = ((my_yh * 4 + x) * 2 + my_core) * NBL + inside
            left = jnp.maximum(block - 1, 0)
            right = jnp.minimum(block + 1, total - 1)
            named = [left, right, block]
            for r in range(RND):
                named.append(owner_ref[block, r] * NBL + offset_ref[block, r])
            for r in range(GLB):
                named.append(global_ref[0, r])
            kv = jnp.concatenate([kv_ref[place(b)] for b in named], axis=0)
            k, v = kv[:, :HD], kv[:, HD:]
            allowed = ((lane < BLK) & (block > 0)) | ((lane >= BLK) & (block < total - 1))
            place_rows = pl.ds(pl.multiple_of(slot * NBL * BLK + inside * BLK, BLK), BLK)
            s = dot32(q_ref[place_rows, :], k, NT) * scale
            s = jnp.concatenate(
                [jnp.where(allowed, s[:, : 2 * BLK], MASKED), s[:, 2 * BLK :]], axis=1
            )
            ks.append(k)
            vs.append(v)
            ss.append(s)
            gps.append(dot32(g_ref[slot, rows, :], v, NT))
        for slot in range(HEADS):
            s, gp = ss[slot], gps[slot]
            e = jnp.exp(s - jnp.max(s, axis=1, keepdims=True))
            p = e * (1.0 / jnp.sum(e, axis=1, keepdims=True))
            delta = jnp.sum(p * gp, axis=1, keepdims=True)
            ds = (p * (gp - delta) * scale).astype(jnp.bfloat16)
            out = dot32(p.astype(jnp.bfloat16), vs[slot], NN).astype(jnp.bfloat16)
            if slot % 2 == 0:
                keep_ref[slot // 2, rows, :] = out
            else:
                near = 1 - odd if slot == 1 else odd
                send_ref[near, rows, :] = out
            gq_ref[slot, rows, :] = dot32(ds, ks[slot], NN).astype(jnp.bfloat16)
        return carry

    lax.fori_loop(0, NBL, step, 0)

    acc = None
    for copy in later:
        copy.wait()
    for slot in range(HEADS):
        term = dot32(gq_ref[slot], t_ref[slot], TN)
        acc = term if acc is None else acc + term
    rows = part_ref.shape[2]
    for z in range(16):
        turned = acc[:, z * HD : (z + 1) * HD].T.astype(jnp.bfloat16)
        for yl in range(2):
            for q in range(4):
                at = yl * 4 * rows + q * rows
                part_ref[((q // 2) * 2 + yl) * 2 + q % 2, z] = turned[at : at + rows]


def attention(where, owners, offsets, global_list, grads, queries, pieces, token_sets):
    smem = pl.BlockSpec(memory_space=pltpu.SMEM)
    vmem = pl.BlockSpec(memory_space=pltpu.VMEM)
    return pl.pallas_call(
        attention_kernel,
        out_shape=(
            jax.ShapeDtypeStruct((2, *grads[0].shape), jnp.bfloat16),
            jax.ShapeDtypeStruct((2, *grads[0].shape), jnp.bfloat16),
            jax.ShapeDtypeStruct((8, 16, 16, HD), jnp.bfloat16),
        ),
        in_specs=[smem] * 4
        + [pl.BlockSpec(memory_space=pl.ANY)] * (1 + HEADS + PIECES + len(token_sets)),
        out_specs=(vmem,) * 3,
        scratch_shapes=[
            pltpu.VMEM((PIECES * PIECE_BLOCKS, BLK, 2 * HD), jnp.bfloat16),
            pltpu.VMEM((HEADS, *grads[0].shape), jnp.bfloat16),
            pltpu.VMEM(queries.shape, jnp.bfloat16),
            pltpu.VMEM((HEADS, *grads[0].shape), jnp.bfloat16),
            pltpu.VMEM((HEADS, *token_sets[0].shape), jnp.bfloat16),
            pltpu.SemaphoreType.DMA((1 + HEADS + PIECES + len(token_sets),)),
        ],
        compiler_params=pltpu.CompilerParams(vmem_limit_bytes=56 * 1024 * 1024),
        name="attention",
    )(where, owners, offsets, global_list, *grads, queries, *pieces, *token_sets)


def merge_kernel(where_ref, keep_ref, next_ref, far_ref, out_ref):
    x = where_ref[1]
    odd, high = lax.rem(x, 2), x // 2
    parts = (keep_ref.at[0], next_ref.at[0], far_ref.at[0], far_ref.at[1])
    for flip, ref in enumerate(parts):
        low = odd if flip % 2 == 0 else 1 - odd
        top = high if flip < 2 else 1 - high
        head = top * 2 + low
        out_ref[:, pl.ds(pl.multiple_of(head * HD, HD), HD)] = ref[...]


def exchanged(block, flip):
    return lax.ppermute(block, "x", [(i, i ^ flip) for i in range(HEADS)])


def per_device(
    tokens, query_weight, key_weight, value_weight, cotangent, rand_owner, rand_offset, global_ids
):
    own = tokens[0]
    count, depth = own.shape
    where = jnp.stack(
        [lax.axis_index("yh"), lax.axis_index("x"), lax.axis_index("core")]
    ).astype(jnp.int32)
    smem = pl.BlockSpec(memory_space=pltpu.SMEM)
    vmem = pl.BlockSpec(memory_space=pltpu.VMEM)

    rows = query_weight.shape[0] // 4
    weight, *grads = pl.pallas_call(
        slice_kernel,
        out_shape=(jax.ShapeDtypeStruct((16, rows, 3 * HD), jnp.bfloat16),)
        + (jax.ShapeDtypeStruct((count, HD), jnp.bfloat16),) * HEADS,
        in_specs=[smem] + [vmem] * 4,
        out_specs=(vmem,) * (1 + HEADS),
        name="slice",
    )(where, key_weight, value_weight, query_weight, cotangent[0])
    weight = lax.all_to_all(weight, "z", 0, 0, tiled=True)

    cut = count // 2
    before, after = shifted(own, "x", 1), shifted(own, "x", -1)
    grads = [grads[0]] + [shifted(grads[h], "x", h) for h in range(1, HEADS)]
    weight, before, after, low_next, high_next, grads[2] = lax.optimization_barrier(
        (weight, before, after, before[:cut], after[cut:], grads[2])
    )
    weight = spread(weight, ("yh", "yl")).reshape(2, 2, 16, rows, 3 * HD)
    partner = [shifted(part, "core", 1) for part in weight]
    low_far, high_far = shifted(low_next, "x", 1), shifted(high_next, "x", -1)
    token_sets = (own, before, after, low_far, high_far)
    kv = project(
        "keys_values", slice(0, 2 * HD), where, weight, *partner, token_sets
    ).reshape(PIECE_BLOCKS, BLK, 2 * HD)
    queries = project(
        "queries", slice(2 * HD, 3 * HD), where, weight, *partner, token_sets
    )
    across = shifted(kv, "yh", 1)
    across, queries, grads[1], grads[3] = lax.optimization_barrier(
        (across, queries, grads[1], grads[3])
    )
    pieces = [kv, shifted(kv, "core", 1), across, shifted(across, "core", 1)]

    kept, sent, partial = attention(
        where, rand_owner[0], rand_offset[0], global_ids, grads, queries, pieces, token_sets
    )
    from_next = exchanged(sent, 1)
    partial = lax.all_to_all(partial, ("yh", "yl", "core"), 0, 0, tiled=True)
    partial = jnp.sum(partial.astype(jnp.float32), axis=0).astype(jnp.bfloat16)
    partial, from_next = lax.optimization_barrier((partial, from_next))
    from_far = exchanged(jnp.stack([kept[1], from_next[1]]), 2)
    partial = lax.all_to_all(partial, "z", 0, 0, tiled=True)
    partial = jnp.sum(partial.astype(jnp.float32), axis=0)
    partial, from_far = lax.optimization_barrier((partial, from_far))
    attn = pl.pallas_call(
        merge_kernel,
        out_shape=jax.ShapeDtypeStruct((count, HEADS * HD), jnp.bfloat16),
        in_specs=[smem] + [vmem] * 3,
        out_specs=vmem,
        name="merge",
    )(where, kept, from_next, from_far)

    final = spread(partial, ("yh", "x", "core")).reshape(2, 4, 2, rows, HD)
    query_grad = final.transpose(0, 2, 3, 1, 4).reshape(4 * rows, HEADS * HD)
    return attn[None], query_grad


def solution(mesh):
    fine = Mesh(
        mesh.devices.reshape(2, 4, 2, 16, 2),
        ("yh", "x", "core", "z", "yl"),
        axis_types=(jax.sharding.AxisType.Auto,) * 5,
    )
    ctx, fsdp = ("yh", "x", "core"), ("z", "yl")
    placed = (
        P(fsdp, ctx, None),
        P(fsdp, None),
        P(fsdp, None),
        P(fsdp, None),
        P(fsdp, ctx, None),
        P(fsdp, None, None),
        P(fsdp, None, None),
        P(fsdp, None),
    )
    return jax.shard_map(
        per_device,
        mesh=fine,
        in_specs=placed,
        out_specs=(P(fsdp, ctx, None), P(fsdp, None)),
        check_vma=False,
    )
```

```python
import functools

import jax
import jax.numpy as jnp
from jax import lax
from jax.experimental import pallas as pl
from jax.experimental.pallas import tpu as pltpu
from jax.sharding import Mesh
from jax.sharding import PartitionSpec as P

HD = 128
BLK = 64
RND = 3
GLB = 2
NBL = 4
PIECE_BLOCKS = 16
PIECES = 4
HEADS = 4
MASKED = -1e30

NT = (((1,), (1,)), ((), ()))
NN = (((1,), (0,)), ((), ()))
TN = (((0,), (0,)), ((), ()))


def dot32(a, b, dims):
    return lax.dot_general(a, b, dims, preferred_element_type=jnp.float32)


def spread(block, axes):
    count = lax.axis_size(axes)
    return lax.all_to_all(
        jnp.broadcast_to(block[None], (count, *block.shape)), axes, 0, 0, tiled=True
    )


def shifted(block, axis, step):
    count = lax.axis_size(axis)
    return lax.ppermute(block, axis, [(i, (i + step) % count) for i in range(count)])


def slice_kernel(where_ref, key_ref, value_ref, query_ref, grad_ref, out_ref, *grad_outs):
    for hop, ref in enumerate(grad_outs):
        head = lax.rem(where_ref[1] + hop, HEADS)
        ref[...] = grad_ref[:, pl.ds(pl.multiple_of(head * HD, HD), HD)]
    count, rows, _ = out_ref.shape
    start = pl.multiple_of((where_ref[0] * 2 + where_ref[2]) * rows, rows)
    col = pl.multiple_of(where_ref[1] * HD, HD)
    for i, ref in enumerate((key_ref, value_ref, query_ref)):
        part = ref[pl.ds(start, rows), pl.ds(col, HD)]
        for copy in range(count):
            out_ref[copy, :, i * HD : (i + 1) * HD] = part


def project_kernel(cols, where_ref, mine_ref, theirs_a_ref, theirs_b_ref, *rest):
    theirs = (theirs_a_ref, theirs_b_ref)
    token_refs, (out_ref, w_ref) = rest[:-2], rest[-2:]
    core = where_ref[2]
    _, _, depth, rows, width = mine_ref.shape

    def assemble(z, carry):
        for yl in range(2):
            for yh in range(2):
                base = (z * 2 + yl) * 4 * rows + yh * 2 * rows
                here = pl.multiple_of(base + core * rows, rows)
                there = pl.multiple_of(base + (1 - core) * rows, rows)
                w_ref[pl.ds(here, rows), :] = mine_ref[yh, yl, z, :, cols]
                w_ref[pl.ds(there, rows), :] = theirs[yh][yl, z, :, cols]
        return carry

    lax.fori_loop(0, depth, assemble, 0)
    for slot, group in token_groups(token_refs):
        tokens = jnp.concatenate([ref[...] for ref in group], axis=0)
        size = tokens.shape[0]
        out = dot32(tokens, w_ref[...], NN).astype(jnp.bfloat16)
        out_ref[slot * size : (slot + 1) * size, :] = out


def token_groups(refs):
    own, before, after, low_far, high_far = refs
    return [(0, (own,)), (1, (before,)), (3, (after,)), (2, (low_far, high_far))]


def project(name, cols, where, mine, theirs_a, theirs_b, token_sets):
    count, depth = token_sets[0].shape
    total, width = count * HEADS, cols.stop - cols.start
    vmem = pl.BlockSpec(memory_space=pltpu.VMEM)
    return pl.pallas_call(
        functools.partial(project_kernel, cols),
        out_shape=jax.ShapeDtypeStruct((total, width), jnp.bfloat16),
        in_specs=[pl.BlockSpec(memory_space=pltpu.SMEM)] + [vmem] * (3 + len(token_sets)),
        out_specs=vmem,
        scratch_shapes=[pltpu.VMEM((depth, width), jnp.bfloat16)],
        compiler_params=pltpu.CompilerParams(vmem_limit_bytes=24 * 1024 * 1024),
        cost_estimate=pl.CostEstimate(
            flops=2 * total * depth * width,
            bytes_accessed=2 * depth * (total + width),
            transcendentals=0,
        ),
        name=name,
    )(where, mine, theirs_a, theirs_b, *token_sets)


def attention_kernel(where_ref, owner_ref, offset_ref, global_ref, *rest):
    given, pieces = rest[: 1 + HEADS], rest[1 + HEADS : 1 + HEADS + PIECES]
    token_refs = rest[1 + HEADS + PIECES : -9]
    keep_ref, send_ref, part_ref, kv_ref, g_ref, q_ref, gq_ref, t_ref, sems = rest[-9:]
    pairs = [
        (piece, kv_ref.at[pl.ds(slot * PIECE_BLOCKS, PIECE_BLOCKS)])
        for slot, piece in enumerate(pieces)
    ]
    pairs += [(ref, g_ref.at[slot]) for slot, ref in enumerate(given[:-1])]
    pairs.append((given[-1], q_ref))
    first = len(pairs)
    for slot, group in token_groups(token_refs):
        size = group[0].shape[0]
        pairs += [
            (ref, t_ref.at[slot, pl.ds(i * size, size)]) for i, ref in enumerate(group)
        ]
    copies = [
        pltpu.make_async_copy(source, target, sems.at[i])
        for i, (source, target) in enumerate(pairs)
    ]
    copies, later = copies[:first], copies[first:]
    for copy in copies:
        copy.start()
    my_yh, my_x, my_core = where_ref[0], where_ref[1], where_ref[2]

    def place(block):
        shard, inside = block // NBL, lax.rem(block, NBL)
        yh, x, core = shard // 8, lax.rem(shard // 2, 4), lax.rem(shard, 2)
        piece = jnp.where(core == my_core, 0, 1) + jnp.where(yh == my_yh, 0, 2)
        slot = lax.rem(my_x + 4 - x, 4)
        return piece * PIECE_BLOCKS + slot * NBL + inside

    for copy in copies:
        copy.wait()
    for copy in later:
        copy.start()

    lane = lax.broadcasted_iota(jnp.int32, (1, 2 * BLK), 1)
    total = PIECES * PIECE_BLOCKS
    scale = HD**-0.5
    odd = lax.rem(my_x, 2)

    def step(inside, carry):
        rows = pl.ds(pl.multiple_of(inside * BLK, BLK), BLK)
        ks, vs, ss, gps = [], [], [], []
        for slot in range(HEADS):
            x = lax.rem(my_x + 4 - slot, 4)
            block = ((my_yh * 4 + x) * 2 + my_core) * NBL + inside
            left = jnp.maximum(block - 1, 0)
            right = jnp.minimum(block + 1, total - 1)
            named = [left, right, block]
            for r in range(RND):
                named.append(owner_ref[block, r] * NBL + offset_ref[block, r])
            for r in range(GLB):
                named.append(global_ref[0, r])
            kv = jnp.concatenate([kv_ref[place(b)] for b in named], axis=0)
            k, v = kv[:, :HD], kv[:, HD:]
            allowed = ((lane < BLK) & (block > 0)) | ((lane >= BLK) & (block < total - 1))
            place_rows = pl.ds(pl.multiple_of(slot * NBL * BLK + inside * BLK, BLK), BLK)
            s = dot32(q_ref[place_rows, :], k, NT) * scale
            s = jnp.concatenate(
                [jnp.where(allowed, s[:, : 2 * BLK], MASKED), s[:, 2 * BLK :]], axis=1
            )
            ks.append(k)
            vs.append(v)
            ss.append(s)
            gps.append(dot32(g_ref[slot, rows, :], v, NT))
        for slot in range(HEADS):
            s, gp = ss[slot], gps[slot]
            e = jnp.exp(s - jnp.max(s, axis=1, keepdims=True))
            p = e * (1.0 / jnp.sum(e, axis=1, keepdims=True))
            delta = jnp.sum(p * gp, axis=1, keepdims=True)
            ds = (p * (gp - delta) * scale).astype(jnp.bfloat16)
            out = dot32(p.astype(jnp.bfloat16), vs[slot], NN).astype(jnp.bfloat16)
            if slot % 2 == 0:
                keep_ref[slot // 2, rows, :] = out
            else:
                near = 1 - odd if slot == 1 else odd
                send_ref[near, rows, :] = out
            gq_ref[slot, rows, :] = dot32(ds, ks[slot], NN).astype(jnp.bfloat16)
        return carry

    lax.fori_loop(0, NBL, step, 0, unroll=True)

    acc = None
    for copy in later:
        copy.wait()
    for slot in range(HEADS):
        term = dot32(gq_ref[slot], t_ref[slot], TN)
        acc = term if acc is None else acc + term
    rows = part_ref.shape[2]
    for z in range(16):
        turned = acc[:, z * HD : (z + 1) * HD].T.astype(jnp.bfloat16)
        for yl in range(2):
            for q in range(4):
                at = yl * 4 * rows + q * rows
                part_ref[((q // 2) * 2 + yl) * 2 + q % 2, z] = turned[at : at + rows]


def attention(where, owners, offsets, global_list, grads, queries, pieces, token_sets):
    smem = pl.BlockSpec(memory_space=pltpu.SMEM)
    vmem = pl.BlockSpec(memory_space=pltpu.VMEM)
    return pl.pallas_call(
        attention_kernel,
        out_shape=(
            jax.ShapeDtypeStruct((2, *grads[0].shape), jnp.bfloat16),
            jax.ShapeDtypeStruct((2, *grads[0].shape), jnp.bfloat16),
            jax.ShapeDtypeStruct((8, 16, 16, HD), jnp.bfloat16),
        ),
        in_specs=[smem] * 4
        + [pl.BlockSpec(memory_space=pl.ANY)] * (1 + HEADS + PIECES + len(token_sets)),
        out_specs=(vmem,) * 3,
        scratch_shapes=[
            pltpu.VMEM((PIECES * PIECE_BLOCKS, BLK, 2 * HD), jnp.bfloat16),
            pltpu.VMEM((HEADS, *grads[0].shape), jnp.bfloat16),
            pltpu.VMEM(queries.shape, jnp.bfloat16),
            pltpu.VMEM((HEADS, *grads[0].shape), jnp.bfloat16),
            pltpu.VMEM((HEADS, *token_sets[0].shape), jnp.bfloat16),
            pltpu.SemaphoreType.DMA((1 + HEADS + PIECES + len(token_sets),)),
        ],
        compiler_params=pltpu.CompilerParams(vmem_limit_bytes=56 * 1024 * 1024),
        name="attention",
    )(where, owners, offsets, global_list, *grads, queries, *pieces, *token_sets)


def merge_kernel(where_ref, keep_ref, next_ref, far_ref, out_ref):
    x = where_ref[1]
    odd, high = lax.rem(x, 2), x // 2
    parts = (keep_ref.at[0], next_ref.at[0], far_ref.at[0], far_ref.at[1])
    for flip, ref in enumerate(parts):
        low = odd if flip % 2 == 0 else 1 - odd
        top = high if flip < 2 else 1 - high
        head = top * 2 + low
        out_ref[:, pl.ds(pl.multiple_of(head * HD, HD), HD)] = ref[...]


def exchanged(block, flip):
    return lax.ppermute(block, "x", [(i, i ^ flip) for i in range(HEADS)])


def per_device(
    tokens, query_weight, key_weight, value_weight, cotangent, rand_owner, rand_offset, global_ids
):
    own = tokens[0]
    count, depth = own.shape
    where = jnp.stack(
        [lax.axis_index("yh"), lax.axis_index("x"), lax.axis_index("core")]
    ).astype(jnp.int32)
    smem = pl.BlockSpec(memory_space=pltpu.SMEM)
    vmem = pl.BlockSpec(memory_space=pltpu.VMEM)

    rows = query_weight.shape[0] // 4
    weight, *grads = pl.pallas_call(
        slice_kernel,
        out_shape=(jax.ShapeDtypeStruct((16, rows, 3 * HD), jnp.bfloat16),)
        + (jax.ShapeDtypeStruct((count, HD), jnp.bfloat16),) * HEADS,
        in_specs=[smem] + [vmem] * 4,
        out_specs=(vmem,) * (1 + HEADS),
        name="slice",
    )(where, key_weight, value_weight, query_weight, cotangent[0])
    weight = lax.all_to_all(weight, "z", 0, 0, tiled=True)

    cut = count // 2
    before, after = shifted(own, "x", 1), shifted(own, "x", -1)
    grads = [grads[0]] + [shifted(grads[h], "x", h) for h in range(1, HEADS)]
    weight, before, after, low_next, high_next, grads[2] = lax.optimization_barrier(
        (weight, before, after, before[:cut], after[cut:], grads[2])
    )
    weight = spread(weight, ("yh", "yl")).reshape(2, 2, 16, rows, 3 * HD)
    partner = [shifted(part, "core", 1) for part in weight]
    low_far, high_far = shifted(low_next, "x", 1), shifted(high_next, "x", -1)
    token_sets = (own, before, after, low_far, high_far)
    kv = project(
        "keys_values", slice(0, 2 * HD), where, weight, *partner, token_sets
    ).reshape(PIECE_BLOCKS, BLK, 2 * HD)
    queries = project(
        "queries", slice(2 * HD, 3 * HD), where, weight, *partner, token_sets
    )
    across = shifted(kv, "yh", 1)
    across, queries, grads[1], grads[3] = lax.optimization_barrier(
        (across, queries, grads[1], grads[3])
    )
    pieces = [kv, shifted(kv, "core", 1), across, shifted(across, "core", 1)]

    kept, sent, partial = attention(
        where, rand_owner[0], rand_offset[0], global_ids, grads, queries, pieces, token_sets
    )
    from_next = exchanged(sent, 1)
    partial = lax.all_to_all(partial, ("yh", "yl", "core"), 0, 0, tiled=True)
    partial = jnp.sum(partial.astype(jnp.float32), axis=0).astype(jnp.bfloat16)
    partial, from_next = lax.optimization_barrier((partial, from_next))
    from_far = exchanged(jnp.stack([kept[1], from_next[1]]), 2)
    partial = lax.all_to_all(partial, "z", 0, 0, tiled=True)
    partial = jnp.sum(partial.astype(jnp.float32), axis=0)
    partial, from_far = lax.optimization_barrier((partial, from_far))
    attn = pl.pallas_call(
        merge_kernel,
        out_shape=jax.ShapeDtypeStruct((count, HEADS * HD), jnp.bfloat16),
        in_specs=[smem] + [vmem] * 3,
        out_specs=vmem,
        name="merge",
    )(where, kept, from_next, from_far)

    final = spread(partial, ("yh", "x", "core")).reshape(2, 4, 2, rows, HD)
    query_grad = final.transpose(0, 2, 3, 1, 4).reshape(4 * rows, HEADS * HD)
    return attn[None], query_grad


def solution(mesh):
    fine = Mesh(
        mesh.devices.reshape(2, 4, 2, 16, 2),
        ("yh", "x", "core", "z", "yl"),
        axis_types=(jax.sharding.AxisType.Auto,) * 5,
    )
    ctx, fsdp = ("yh", "x", "core"), ("z", "yl")
    placed = (
        P(fsdp, ctx, None),
        P(fsdp, None),
        P(fsdp, None),
        P(fsdp, None),
        P(fsdp, ctx, None),
        P(fsdp, None, None),
        P(fsdp, None, None),
        P(fsdp, None),
    )
    return jax.shard_map(
        per_device,
        mesh=fine,
        in_specs=placed,
        out_specs=(P(fsdp, ctx, None), P(fsdp, None)),
        check_vma=False,
    )
```
